512 devices in a mesh: wide: 32 (over x_lo, z), narrow: 16 (over y, x_hi, core).
Axes of the slice: x: 4 (x_hi: 2, x_lo: 2; x = x_hi * 2 + x_lo), y: 4, z: 16, core: 2. Of those that a mesh axis runs over, the one named last changes fastest.
Arguments:
- batch: float32 [512, 768], P('wide'), may hold values from -9 to 9
- targets: float32 [512, 512], P(('wide', 'narrow')), may hold values from -6 to 6
- centers: float32 [65536, 768], P(('wide', 'narrow')), may hold values from -9 to 9
- weights: float32 [65536, 512], P(('wide', 'narrow')), may hold values from -6 to 6
Outputs:
- residual: float32 [512, 512], P(('wide', 'narrow'))
- new_weights: float32 [65536, 512], P(('wide', 'narrow'))
The draws below stay inside these ranges and needn't reach their ends.
All inputs are finite; a program needn't handle non-finite values.
Results may differ from the reference program's by a relative error of at most 0.0001.
Values sent between devices are 32-bit elements; how exact they have to be, the bound alone decides.
A program may use at most 64 MiB of HBM per device.

```python
import jax
import jax.numpy as jnp
from jax import lax

D = 768
C = 512
M_DEV = 128
CENTERS = 65536
ROWS = 512


cluster_count = 16


latent_dims = 8


mean_spread = 1.58


latent_spread = 0.245


noise_spread = 0.5


def shared_layout(key):
    mean_key = jax.random.fold_in(key, 9101)
    map_key = jax.random.fold_in(key, 9102)
    means = jax.random.normal(mean_key, (cluster_count, D), jnp.float32) * mean_spread
    mapping = jax.random.normal(map_key, (latent_dims, D), jnp.float32)
    return (means, mapping)


def place_points(key, salt, count):
    means, mapping = shared_layout(key)
    own_key = jax.random.fold_in(key, salt)
    label_key, latent_key, noise_key = jax.random.split(own_key, 3)
    labels = jax.random.randint(label_key, (count,), 0, cluster_count)
    latent = jax.random.normal(latent_key, (count, latent_dims), jnp.float32) * latent_spread
    noise = jax.random.normal(noise_key, (count, D), jnp.float32) * noise_spread
    points = means[labels] + jnp.dot(latent, mapping) + noise
    return jnp.clip(points, -9.0, 9.0).astype(jnp.float32)


def draw_batch(key, part):
    return place_points(key, 7301, ROWS)


def draw_centers(key, part):
    return place_points(key, 7302, CENTERS)


def steps_of(rng, dims, pieces, least, top_value):
    loudness = 1.0
    for position, shards_of in pieces:
        heights = jax.random.uniform(jax.random.fold_in(jax.random.fold_in(rng, 6), position), (shards_of,), jnp.float32, least / len(pieces), top_value / len(pieces))
        loudness = loudness * jnp.repeat(jnp.exp(heights), dims[position] // shards_of).reshape((-1,) + (1,) * (len(dims) - 1 - position))
    return loudness


def normal_values(stream_key, dims, width, bound, cuts=(), held_as=jnp.bfloat16):
    values = jax.random.normal(stream_key, dims, jnp.float32) * width
    if len(cuts) > 0:
        values = steps_of(stream_key, dims, cuts, -0.22, 0.18) * values
    return jnp.clip(values, min=-bound, max=bound).astype(held_as)


def setup_inputs(seed: int = 0) -> dict:
    seeds = jax.random.split(jax.random.key(seed), 5)
    batch = draw_batch(jax.random.fold_in(seeds[4], 71), 0)
    targets = normal_values(seeds[1], (ROWS, C), 1.0, 6.0, ((0, 512),), jnp.float32)
    centers = draw_centers(jax.random.fold_in(seeds[4], 71), 0)
    weights = normal_values(seeds[3], (CENTERS, C), 1.0, 6.0, ((0, 512),), jnp.float32)
    return dict(batch=batch, targets=targets, centers=centers, weights=weights)


def kernel_block(points, center_rows):
    row_norms = lax.optimization_barrier(jnp.sum(points * points, axis=1))
    center_norms = lax.optimization_barrier(jnp.sum(center_rows * center_rows, axis=1))
    cross = jnp.dot(points, center_rows.T, precision=lax.Precision.HIGHEST, preferred_element_type=jnp.float32)
    return jnp.exp(-(row_norms[:, None] + center_norms[None, :] - 2.0 * cross) / D)

def reference(batch, targets, centers, weights):
    blocks = CENTERS // M_DEV
    center_blocks = centers.reshape(blocks, M_DEV, D)
    weight_blocks = weights.reshape(blocks, M_DEV, C)
    kernel = lax.map(lambda block: kernel_block(batch, block), center_blocks)

    def accumulate(total, pair):
        return (total + jnp.dot(pair[0], pair[1], precision=lax.Precision.HIGHEST, preferred_element_type=jnp.float32), None)
    start_sum = jnp.zeros((ROWS, C), jnp.float32)
    summed, _ = lax.scan(accumulate, start_sum, (kernel, weight_blocks))
    prediction = summed * (8.0 / jnp.sqrt(jnp.float32(CENTERS)))
    residual = prediction - targets

    def update(pair):
        change = jnp.dot(pair[0].T, residual, precision=lax.Precision.HIGHEST, preferred_element_type=jnp.float32)
        return pair[1] - 32.0 / ROWS * change
    new_blocks = lax.map(update, (kernel, weight_blocks))
    return (residual, new_blocks.reshape(CENTERS, C))
```

```python
import functools
import math

import jax
import jax.numpy as jnp
from jax import lax
from jax.experimental import pallas as pl
from jax.experimental.pallas import tpu as pltpu
from jax.sharding import PartitionSpec as P

SIDE, DEPTH, CORES = 4, 16, 2
PLANE = SIDE * SIDE
GROUP = 8
NEAR = 4
MESH = pl.DeviceIdType.MESH
HI = lax.Precision.HIGHEST


def place():
    w, n = lax.axis_index("wide"), lax.axis_index("narrow")
    core, rest = lax.rem(n, CORES), lax.div(n, CORES)
    x_lo, z = lax.div(w, DEPTH), lax.rem(w, DEPTH)
    x_hi, y = lax.rem(rest, 2), lax.div(rest, 2)
    return x_hi * 2 + x_lo, y, z, core, n


def name_of(x, y, z, core):
    return (lax.rem(x, 2) * DEPTH + z, (y * 2 + lax.div(x, 2)) * CORES + core)


def body(
    pred_scale, step, batch_ref, targets_ref, centers_ref, weights_ref, res_ref, new_ref,
    xb, tg, cc, ww, z1, xa, cn, kk, pp, cb, s3, zb, rz, rb, uu, ub,
    lsem, core_s, core_r, az_s, az_r, ap_s, ap_r, cp_s, cp_r, cz_s, cz_r, dz_s, dz_r, dp_s, dp_r,
):
    x, y, z, core, n = place()
    features = cc.shape[2]
    m = cc.shape[1]
    lanes = 128
    xk = features // lanes
    rk = rb.shape[1] // lanes

    loads = [
        pltpu.make_async_copy(batch_ref, xb, lsem.at[0]),
        pltpu.make_async_copy(targets_ref, tg, lsem.at[1]),
        pltpu.make_async_copy(centers_ref, cc.at[0], lsem.at[2]),
        pltpu.make_async_copy(weights_ref, ww.at[0], lsem.at[3]),
    ]
    for load in loads:
        load.start()

    mate = name_of(x, y, z, 1 - core)
    z_peers = {d: name_of(x, y, lax.rem(z + d, DEPTH), core) for d in range(1, DEPTH)}
    p_peers = {
        q: name_of(lax.rem(x + q // SIDE, SIDE), lax.rem(y + q % SIDE, SIDE), z, core)
        for q in range(1, PLANE)
    }
    everyone = [mate, *z_peers.values(), *p_peers.values()]
    barrier = pltpu.get_barrier_semaphore()
    for peer in everyone:
        pl.semaphore_signal(barrier, inc=1, device_id=peer, device_id_type=MESH)

    def remote(src, dst, send, recv, peer):
        return pltpu.make_async_remote_copy(
            src_ref=src, dst_ref=dst, send_sem=send, recv_sem=recv,
            device_id=peer, device_id_type=MESH,
        )

    def opposite(q):
        return (-(q // SIDE)) % SIDE * SIDE + (-(q % SIDE)) % SIDE

    far_first = sorted(range(1, DEPTH), key=lambda d: -min(d, DEPTH - d))

    loads[0].wait()
    mine = xb[pl.ds(n, 1), :]
    for k in range(xk):
        z1[NEAR, k : k + 1, :] = mine[:, k * lanes : (k + 1) * lanes]
    loads[2].wait()
    loads[3].wait()
    loads[1].wait()
    pl.semaphore_wait(barrier, len(everyone))

    az = {
        d: remote(
            z1.at[NEAR], z1.at[(NEAR - d) % DEPTH], az_s.at[d], az_r.at[(NEAR - d) % DEPTH], z_peers[d]
        )
        for d in range(1, DEPTH)
    }
    for d in far_first:
        az[d].start()
    swap_c = remote(cc.at[0], cc.at[1], core_s.at[0], core_r.at[0], mate)
    swap_w = remote(ww.at[0], ww.at[1], core_s.at[1], core_r.at[1], mate)
    swap_c.start()
    swap_w.start()

    def landed_z(copies, s):
        copies[(NEAR - s) % DEPTH].wait_recv()

    ap = {}
    for g in range(2):
        rows = slice(g * GROUP, (g + 1) * GROUP)
        for s in range(g * GROUP, (g + 1) * GROUP):
            if s != NEAR:
                landed_z(az, s)
        for k in range(xk):
            xa[0, rows, k * lanes : (k + 1) * lanes] = z1[rows, k, :]
        for q in range(1, PLANE):
            ap[g, q] = remote(
                xa.at[0, pl.ds(g * GROUP, GROUP)],
                xa.at[opposite(q), pl.ds(g * GROUP, GROUP)],
                ap_s.at[g, q], ap_r.at[g, opposite(q)], p_peers[q],
            )
            ap[g, q].start()

    swap_c.wait_recv()
    both = cc[...].reshape(2 * m, features)
    ones = jnp.ones((8, features), jnp.float32)
    cn[...] = lax.dot_general(
        ones, both * both, (((1,), (1,)), ((), ())), precision=HI, preferred_element_type=jnp.float32
    )
    swap_w.wait_recv()

    cp = {}
    for g in range(2):
        rows = slice(g * GROUP, (g + 1) * GROUP)
        for q in range(1, PLANE):
            ap[g, opposite(q)].wait_recv()
        points = xa[:, rows, :].reshape(PLANE * GROUP, features)
        norms = jnp.sum(points * points, axis=1, keepdims=True)
        cross = lax.dot_general(
            points, cc[...].reshape(2 * m, features), (((1,), (1,)), ((), ())),
            precision=HI, preferred_element_type=jnp.float32,
        )
        kernel = jnp.exp(-(norms + cn[0:1, :] - 2.0 * cross) / features)
        kk[:, rows, :] = kernel.reshape(PLANE, GROUP, 2 * m)
        part = jnp.dot(
            kernel, ww[...].reshape(2 * m, -1), precision=HI, preferred_element_type=jnp.float32
        )
        pp[:, rows, :] = part.reshape(PLANE, GROUP, -1)
        for q in range(1, PLANE):
            cp[g, q] = remote(
                pp.at[q, pl.ds(g * GROUP, GROUP)],
                cb.at[opposite(q), pl.ds(g * GROUP, GROUP)],
                cp_s.at[g, q], cp_r.at[g, opposite(q)], p_peers[q],
            )
            cp[g, q].start()

    cz = {}
    for g in range(2):
        rows = slice(g * GROUP, (g + 1) * GROUP)
        for q in range(1, PLANE):
            cp[g, opposite(q)].wait_recv()
        total = pp[0, rows, :]
        for q in range(1, PLANE):
            total = total + cb[q, rows, :]
        for k in range(rk):
            s3[rows, k, :] = total[:, k * lanes : (k + 1) * lanes]
        for s in range(g * GROUP, (g + 1) * GROUP):
            d = (s - NEAR) % DEPTH
            if d:
                cz[d] = remote(
                    s3.at[s], zb.at[(NEAR - d) % DEPTH], cz_s.at[d], cz_r.at[(NEAR - d) % DEPTH], z_peers[d]
                )
                cz[d].start()

    own = s3[NEAR]
    for s in range(DEPTH):
        if s != NEAR:
            landed_z(cz, s)
            own = own + zb[s]
    own = own * pred_scale
    for k in range(rk):
        piece = own[k : k + 1, :] - tg[:, k * lanes : (k + 1) * lanes]
        rz[NEAR, k : k + 1, :] = piece
        res_ref[:, k * lanes : (k + 1) * lanes] = piece

    dz = {
        d: remote(
            rz.at[NEAR], rz.at[(NEAR - d) % DEPTH], dz_s.at[d], dz_r.at[(NEAR - d) % DEPTH], z_peers[d]
        )
        for d in range(1, DEPTH)
    }
    for d in far_first:
        dz[d].start()

    dp = {}
    for g in range(2):
        rows = slice(g * GROUP, (g + 1) * GROUP)
        for s in range(g * GROUP, (g + 1) * GROUP):
            if s != NEAR:
                landed_z(dz, s)
        for k in range(rk):
            rb[rows, k * lanes : (k + 1) * lanes] = rz[rows, k, :]
        for q in range(1, PLANE):
            here = pl.ds(g * GROUP, GROUP)
            there = pl.ds(opposite(q) * DEPTH + g * GROUP, GROUP)
            dp[g, q] = remote(
                rb.at[here], rb.at[there], dp_s.at[g, q], dp_r.at[g, opposite(q)], p_peers[q]
            )
            dp[g, q].start()

    for g in range(2):
        for q in range(1, PLANE):
            dp[g, opposite(q)].wait_recv()
    uu[...] = lax.dot_general(
        kk[...].reshape(PLANE * DEPTH, 2 * m), rb[...], (((0,), (0,)), ((), ())),
        precision=HI, preferred_element_type=jnp.float32,
    )
    swap_u = remote(uu.at[pl.ds(m, m)], ub, core_s.at[2], core_r.at[2], mate)
    swap_u.start()
    swap_u.wait_recv()
    new_ref[...] = ww[0] - step * (uu[0:m, :] + ub[...])

    swap_c.wait_send()
    swap_w.wait_send()
    swap_u.wait_send()
    for copies in (az, ap, cp, cz, dz, dp):
        for copy in copies.values():
            copy.wait_send()


def shards(batch, targets, centers, weights):
    m, features = centers.shape
    outputs = weights.shape[1]
    devices = lax.axis_size("wide") * lax.axis_size("narrow")
    all_rows = batch.shape[0] * lax.axis_size("wide")
    pred_scale = 8.0 / math.sqrt(m * devices)
    f32 = jnp.float32
    vmem = pltpu.VMEM
    dma = pltpu.SemaphoreType.DMA
    xk, rk = features // 128, outputs // 128
    rows = PLANE * DEPTH
    scratch = [
        vmem(batch.shape, f32),
        vmem(targets.shape, f32),
        vmem((2, m, features), f32),
        vmem((2, m, outputs), f32),
        vmem((DEPTH, xk, 128), f32),
        vmem((PLANE, DEPTH, features), f32),
        vmem((8, 2 * m), f32),
        vmem((PLANE, DEPTH, 2 * m), f32),
        vmem((PLANE, DEPTH, outputs), f32),
        vmem((PLANE, DEPTH, outputs), f32),
        vmem((DEPTH, rk, 128), f32),
        vmem((DEPTH, rk, 128), f32),
        vmem((DEPTH, rk, 128), f32),
        vmem((rows, outputs), f32),
        vmem((2 * m, outputs), f32),
        vmem((m, outputs), f32),
        dma((4,)),
        dma((3,)), dma((3,)),
        dma((DEPTH,)), dma((DEPTH,)),
        dma((2, PLANE)), dma((2, PLANE)),
        dma((2, PLANE)), dma((2, PLANE)),
        dma((DEPTH,)), dma((DEPTH,)),
        dma((DEPTH,)), dma((DEPTH,)),
        dma((2, PLANE)), dma((2, PLANE)),
    ]
    return pl.pallas_call(
        functools.partial(body, pred_scale, 32.0 / all_rows),
        out_shape=(
            jax.ShapeDtypeStruct(targets.shape, f32),
            jax.ShapeDtypeStruct(weights.shape, f32),
        ),
        in_specs=[pl.BlockSpec(memory_space=pl.ANY)] * 4,
        out_specs=(pl.BlockSpec(memory_space=pltpu.VMEM),) * 2,
        scratch_shapes=scratch,
        compiler_params=pltpu.CompilerParams(
            collective_id=0, has_side_effects=True, vmem_limit_bytes=50 << 20
        ),
    )(batch, targets, centers, weights)


def solution(mesh):
    both = P(("wide", "narrow"), None)
    return jax.shard_map(
        shards, mesh=mesh, in_specs=(P("wide", None), both, both, both), out_specs=(both, both), check_vma=False
    )
```

```python
import functools
import math

import jax
import jax.numpy as jnp
from jax import lax
from jax.experimental import pallas as pl
from jax.experimental.pallas import tpu as pltpu
from jax.sharding import PartitionSpec as P

SIDE, DEPTH, CORES = 4, 16, 2
PLANE = SIDE * SIDE
GROUP = 8
REACH = 4
NEAR = 4
MESH = pl.DeviceIdType.MESH
HI = lax.Precision.HIGHEST


def place():
    w, n = lax.axis_index("wide"), lax.axis_index("narrow")
    core, rest = lax.rem(n, CORES), lax.div(n, CORES)
    x_lo, z = lax.div(w, DEPTH), lax.rem(w, DEPTH)
    x_hi, y = lax.rem(rest, 2), lax.div(rest, 2)
    return x_hi * 2 + x_lo, y, z, core, n


def name_of(x, y, z, core):
    return (lax.rem(x, 2) * DEPTH + z, (y * 2 + lax.div(x, 2)) * CORES + core)


def body(
    pred_scale, step, batch_ref, targets_ref, centers_ref, weights_ref, res_ref, new_ref,
    xb, tg, cc, ww, z1, xa, cn, kk, pp, cb, s3, zb, rz, rb, uu, ub,
    lsem, core_s, core_r, az_s, az_r, ap_s, ap_r, cp_s, cp_r, cz_s, cz_r, dz_s, dz_r, dp_s, dp_r,
):
    x, y, z, core, n = place()
    features = cc.shape[2]
    m = cc.shape[1]
    lanes = 128
    xk = features // lanes
    rk = rb.shape[2] // lanes

    loads = [
        pltpu.make_async_copy(batch_ref, xb, lsem.at[0]),
        pltpu.make_async_copy(targets_ref, tg, lsem.at[1]),
        pltpu.make_async_copy(centers_ref, cc.at[0], lsem.at[2]),
        pltpu.make_async_copy(weights_ref, ww.at[0], lsem.at[3]),
    ]
    for load in loads:
        load.start()

    mate = name_of(x, y, z, 1 - core)
    z_peers = {d: name_of(x, y, lax.rem(z + d, DEPTH), core) for d in range(1, DEPTH)}
    p_peers = {
        q: name_of(lax.rem(x + q // SIDE, SIDE), lax.rem(y + q % SIDE, SIDE), z, core)
        for q in range(1, PLANE)
    }
    greeted = [mate, *p_peers.values()]
    greeted += [z_peers[d % DEPTH] for d in range(-REACH, REACH + 1) if d]
    barrier = pltpu.get_barrier_semaphore()
    for peer in greeted:
        pl.semaphore_signal(barrier, inc=1, device_id=peer, device_id_type=MESH)

    def remote(src, dst, send, recv, peer):
        return pltpu.make_async_remote_copy(
            src_ref=src, dst_ref=dst, send_sem=send, recv_sem=recv,
            device_id=peer, device_id_type=MESH,
        )

    sent = []

    def go(copy):
        copy.start()
        sent.append(copy)

    def arrive(copy):
        copy.wait_recv()

    def opposite(q):
        return (-(q // SIDE)) % SIDE * SIDE + (-(q % SIDE)) % SIDE

    far_first = sorted(range(1, DEPTH), key=lambda d: -min(d, DEPTH - d))

    loads[0].wait()
    mine = xb[pl.ds(n, 1), :]
    for k in range(xk):
        z1[NEAR, k : k + 1, :] = mine[:, k * lanes : (k + 1) * lanes]
    pl.semaphore_wait(barrier, len(greeted))

    az = {}

    def along_z(source, d, slot):
        az[slot] = remote(z1.at[source], z1.at[slot], az_s.at[slot], az_r.at[slot], z_peers[d % DEPTH])
        go(az[slot])

    for d in (4, -4, 3, -3, 2, -2, 1, -1):
        along_z(NEAR, d, NEAR - d)
    loads[2].wait()
    swap_c = remote(cc.at[0], cc.at[1], core_s.at[0], core_r.at[0], mate)
    go(swap_c)
    loads[3].wait()
    swap_w = remote(ww.at[0], ww.at[1], core_s.at[1], core_r.at[1], mate)
    go(swap_w)
    for s in (3, 5, 2, 6, 1, 7, 0):
        arrive(az[s])
        if s < NEAR:
            along_z(s, REACH, s + 12)
        else:
            along_z(s, -REACH, s + 4)

    ap = {}
    for g in range(2):
        rows = slice(g * GROUP, (g + 1) * GROUP)
        if g == 1:
            for s in range(GROUP, DEPTH):
                arrive(az[s])
        for k in range(xk):
            xa[0, rows, k * lanes : (k + 1) * lanes] = z1[rows, k, :]
        for q in range(1, PLANE):
            ap[g, q] = remote(
                xa.at[0, pl.ds(g * GROUP, GROUP)],
                xa.at[opposite(q), pl.ds(g * GROUP, GROUP)],
                ap_s.at[g, q], ap_r.at[g, opposite(q)], p_peers[q],
            )
            go(ap[g, q])

    def landed_z(copies, s):
        arrive(copies[(NEAR - s) % DEPTH])

    loads[1].wait()
    arrive(swap_c)
    both = cc[...].reshape(2 * m, features)
    ones = jnp.ones((8, features), jnp.float32)
    cn[...] = lax.dot_general(
        ones, both * both, (((1,), (1,)), ((), ())), precision=HI, preferred_element_type=jnp.float32
    )
    arrive(swap_w)

    cp = {}
    for g in range(2):
        rows = slice(g * GROUP, (g + 1) * GROUP)
        for q in range(1, PLANE):
            arrive(ap[g, opposite(q)])
        points = xa[:, rows, :].reshape(PLANE * GROUP, features)
        norms = jnp.sum(points * points, axis=1, keepdims=True)
        cross = lax.dot_general(
            points, cc[...].reshape(2 * m, features), (((1,), (1,)), ((), ())),
            precision=HI, preferred_element_type=jnp.float32,
        )
        kernel = jnp.exp(-(norms + cn[0:1, :] - 2.0 * cross) / features)
        kk[:, rows, :] = kernel.reshape(PLANE, GROUP, 2 * m)
        part = jnp.dot(
            kernel, ww[...].reshape(2 * m, -1), precision=HI, preferred_element_type=jnp.float32
        )
        pp[:, rows, :] = part.reshape(PLANE, GROUP, -1)
        for q in range(1, PLANE):
            cp[g, q] = remote(
                pp.at[q, pl.ds(g * GROUP, GROUP)],
                cb.at[opposite(q), pl.ds(g * GROUP, GROUP)],
                cp_s.at[g, q], cp_r.at[g, opposite(q)], p_peers[q],
            )
            go(cp[g, q])

    cz = {}
    for g in range(2):
        rows = slice(g * GROUP, (g + 1) * GROUP)
        for q in range(1, PLANE):
            arrive(cp[g, opposite(q)])
        total = pp[0, rows, :]
        for q in range(1, PLANE):
            total = total + cb[q, rows, :]
        for k in range(rk):
            s3[rows, k, :] = total[:, k * lanes : (k + 1) * lanes]
        for s in range(g * GROUP, (g + 1) * GROUP):
            d = (s - NEAR) % DEPTH
            if d:
                cz[d] = remote(
                    s3.at[s], zb.at[(NEAR - d) % DEPTH], cz_s.at[d], cz_r.at[(NEAR - d) % DEPTH], z_peers[d]
                )
                go(cz[d])

    own = s3[NEAR]
    for s in range(DEPTH):
        if s != NEAR:
            landed_z(cz, s)
            own = own + zb[s]
    own = own * pred_scale
    for k in range(rk):
        piece = own[k : k + 1, :] - tg[:, k * lanes : (k + 1) * lanes]
        rz[NEAR, k : k + 1, :] = piece
        res_ref[:, k * lanes : (k + 1) * lanes] = piece

    dz = {
        d: remote(
            rz.at[NEAR], rz.at[(NEAR - d) % DEPTH], dz_s.at[d], dz_r.at[(NEAR - d) % DEPTH], z_peers[d]
        )
        for d in range(1, DEPTH)
    }
    for d in far_first:
        go(dz[d])

    dp = {}
    for g in range(2):
        rows = slice(g * GROUP, (g + 1) * GROUP)
        for s in range(g * GROUP, (g + 1) * GROUP):
            if s != NEAR:
                landed_z(dz, s)
        for k in range(rk):
            rb[0, rows, k * lanes : (k + 1) * lanes] = rz[rows, k, :]
        for q in range(1, PLANE):
            dp[g, q] = remote(
                rb.at[0, pl.ds(g * GROUP, GROUP)],
                rb.at[opposite(q), pl.ds(g * GROUP, GROUP)],
                dp_s.at[g, q], dp_r.at[g, opposite(q)], p_peers[q],
            )
            go(dp[g, q])

    change = None
    for g in range(2):
        rows = slice(g * GROUP, (g + 1) * GROUP)
        for q in range(1, PLANE):
            arrive(dp[g, opposite(q)])
        term = lax.dot_general(
            kk[:, rows, :].reshape(PLANE * GROUP, 2 * m),
            rb[:, rows, :].reshape(PLANE * GROUP, -1),
            (((0,), (0,)), ((), ())), precision=HI, preferred_element_type=jnp.float32,
        )
        change = term if change is None else change + term
    uu[...] = change
    swap_u = remote(uu.at[pl.ds(m, m)], ub, core_s.at[2], core_r.at[2], mate)
    go(swap_u)
    arrive(swap_u)
    new_ref[...] = ww[0] - step * (uu[0:m, :] + ub[...])

    for copy in sent:
        copy.wait_send()


def shards(batch, targets, centers, weights):
    m, features = centers.shape
    outputs = weights.shape[1]
    devices = lax.axis_size("wide") * lax.axis_size("narrow")
    all_rows = batch.shape[0] * lax.axis_size("wide")
    pred_scale = 8.0 / math.sqrt(m * devices)
    f32 = jnp.float32
    vmem = pltpu.VMEM
    dma = pltpu.SemaphoreType.DMA
    xk, rk = features // 128, outputs // 128
    scratch = [
        vmem(batch.shape, f32),
        vmem(targets.shape, f32),
        vmem((2, m, features), f32),
        vmem((2, m, outputs), f32),
        vmem((DEPTH, xk, 128), f32),
        vmem((PLANE, DEPTH, features), f32),
        vmem((8, 2 * m), f32),
        vmem((PLANE, DEPTH, 2 * m), f32),
        vmem((PLANE, DEPTH, outputs), f32),
        vmem((PLANE, DEPTH, outputs), f32),
        vmem((DEPTH, rk, 128), f32),
        vmem((DEPTH, rk, 128), f32),
        vmem((DEPTH, rk, 128), f32),
        vmem((PLANE, DEPTH, outputs), f32),
        vmem((2 * m, outputs), f32),
        vmem((m, outputs), f32),
        dma((4,)),
        dma((3,)), dma((3,)),
        dma((DEPTH,)), dma((DEPTH,)),
        dma((2, PLANE)), dma((2, PLANE)),
        dma((2, PLANE)), dma((2, PLANE)),
        dma((DEPTH,)), dma((DEPTH,)),
        dma((DEPTH,)), dma((DEPTH,)),
        dma((2, PLANE)), dma((2, PLANE)),
    ]
    return pl.pallas_call(
        functools.partial(body, pred_scale, 32.0 / all_rows),
        out_shape=(
            jax.ShapeDtypeStruct(targets.shape, f32),
            jax.ShapeDtypeStruct(weights.shape, f32),
        ),
        in_specs=[pl.BlockSpec(memory_space=pltpu.HBM)] * 4,
        out_specs=(pl.BlockSpec(memory_space=pltpu.VMEM),) * 2,
        scratch_shapes=scratch,
        compiler_params=pltpu.CompilerParams(
            collective_id=0, has_side_effects=True, vmem_limit_bytes=(64 << 20) - (160 << 10)
        ),
    )(batch, targets, centers, weights)


def solution(mesh):
    both = P(("wide", "narrow"), None)
    return jax.shard_map(
        shards, mesh=mesh, in_specs=(P("wide", None), both, both, both), out_specs=(both, both), check_vma=False
    )
```

```python
import functools
import math

import jax
import jax.numpy as jnp
from jax import lax
from jax.experimental import pallas as pl
from jax.experimental.pallas import tpu as pltpu
from jax.sharding import PartitionSpec as P

SIDE, DEPTH, CORES = 4, 16, 2
PLANE = SIDE * SIDE
GROUP = 8
REACH = 4
NEAR = 4
MESH = pl.DeviceIdType.MESH
HI = lax.Precision.HIGHEST


def place():
    w, n = lax.axis_index("wide"), lax.axis_index("narrow")
    core, rest = lax.rem(n, CORES), lax.div(n, CORES)
    x_lo, z = lax.div(w, DEPTH), lax.rem(w, DEPTH)
    x_hi, y = lax.rem(rest, 2), lax.div(rest, 2)
    return x_hi * 2 + x_lo, y, z, core, n


def name_of(x, y, z, core):
    return (lax.rem(x, 2) * DEPTH + z, (y * 2 + lax.div(x, 2)) * CORES + core)


def hops(d):
    return min(d, SIDE - d)


def body(
    pred_scale, step, batch_ref, targets_ref, centers_ref, weights_ref, res_ref, new_ref,
    xb, tg, cc, ww, z1, xa, cn, kk, pp, cb, s3, zb, rz, rb, uu, ub,
    lsem, core_s, core_r, az_s, az_r, ap_s, ap_r, cp_s, cp_r, cz_s, cz_r, dz_s, dz_r, dp_s, dp_r,
):
    x, y, z, core, n = place()
    features = cc.shape[2]
    m = cc.shape[1]
    lanes = 128
    xk = features // lanes
    rk = rb.shape[2] // lanes

    loads = [
        pltpu.make_async_copy(batch_ref, xb, lsem.at[0]),
        pltpu.make_async_copy(targets_ref, tg, lsem.at[1]),
        pltpu.make_async_copy(centers_ref, cc.at[0], lsem.at[2]),
        pltpu.make_async_copy(weights_ref, ww.at[0], lsem.at[3]),
    ]
    for load in loads:
        load.start()

    mate = name_of(x, y, z, 1 - core)
    z_peers = {d: name_of(x, y, lax.rem(z + d, DEPTH), core) for d in range(1, DEPTH)}
    p_peers = {
        q: name_of(lax.rem(x + q // SIDE, SIDE), lax.rem(y + q % SIDE, SIDE), z, core)
        for q in range(1, PLANE)
    }
    greeted = [mate, *p_peers.values()]
    greeted += [z_peers[d % DEPTH] for d in range(-REACH, REACH + 1) if d]
    barrier = pltpu.get_barrier_semaphore()
    for peer in greeted:
        pl.semaphore_signal(barrier, inc=1, device_id=peer, device_id_type=MESH)

    def remote(src, dst, send, recv, peer):
        return pltpu.make_async_remote_copy(
            src_ref=src, dst_ref=dst, send_sem=send, recv_sem=recv,
            device_id=peer, device_id_type=MESH,
        )

    sent = []

    def go(copy):
        copy.start()
        sent.append(copy)

    def arrive(copy):
        copy.wait_recv()

    def got(copy):
        copy.wait()

    def opposite(q):
        return (-(q // SIDE)) % SIDE * SIDE + (-(q % SIDE)) % SIDE

    far_first = sorted(range(1, DEPTH), key=lambda d: -min(d, DEPTH - d))
    plane_far_first = sorted(range(1, PLANE), key=lambda q: -hops(q // SIDE) - hops(q % SIDE))

    got(loads[0])
    mine = xb[pl.ds(n, 1), :]
    for k in range(xk):
        z1[NEAR, k : k + 1, :] = mine[:, k * lanes : (k + 1) * lanes]
    pl.semaphore_wait(barrier, len(greeted))

    az = {}

    def along_z(source, d, slot):
        az[slot] = remote(z1.at[source], z1.at[slot], az_s.at[slot], az_r.at[slot], z_peers[d % DEPTH])
        go(az[slot])

    for d in (4, -4, 3, -3, 2, -2, 1, -1):
        along_z(NEAR, d, NEAR - d)
    got(loads[2])
    swap_c = remote(cc.at[0], cc.at[1], core_s.at[0], core_r.at[0], mate)
    go(swap_c)
    got(loads[3])
    swap_w = remote(ww.at[0], ww.at[1], core_s.at[1], core_r.at[1], mate)
    go(swap_w)
    for s in (3, 5, 2, 6, 1, 7, 0):
        arrive(az[s])
        if s < NEAR:
            along_z(s, REACH, s + 12)
        else:
            along_z(s, -REACH, s + 4)

    ap = {}
    for g in range(2):
        rows = slice(g * GROUP, (g + 1) * GROUP)
        if g == 1:
            for s in range(GROUP, DEPTH):
                arrive(az[s])
        for k in range(xk):
            xa[0, rows, k * lanes : (k + 1) * lanes] = z1[rows, k, :]
        for q in plane_far_first:
            ap[g, q] = remote(
                xa.at[0, pl.ds(g * GROUP, GROUP)],
                xa.at[opposite(q), pl.ds(g * GROUP, GROUP)],
                ap_s.at[g, q], ap_r.at[g, opposite(q)], p_peers[q],
            )
            go(ap[g, q])

    def landed_z(copies, s):
        arrive(copies[(NEAR - s) % DEPTH])

    got(loads[1])
    arrive(swap_c)
    both = cc[...].reshape(2 * m, features)
    ones = jnp.ones((8, features), jnp.float32)
    cn[...] = lax.dot_general(
        ones, both * both, (((1,), (1,)), ((), ())), precision=HI, preferred_element_type=jnp.float32
    )
    arrive(swap_w)

    cp = {}

    def send_parts(g):
        for q in plane_far_first:
            cp[g, q] = remote(
                pp.at[q, pl.ds(g * GROUP, GROUP)],
                cb.at[opposite(q), pl.ds(g * GROUP, GROUP)],
                cp_s.at[g, q], cp_r.at[g, opposite(q)], p_peers[q],
            )
            go(cp[g, q])

    for g in range(2):
        rows = slice(g * GROUP, (g + 1) * GROUP)
        for q in range(1, PLANE):
            arrive(ap[g, opposite(q)])
        if g == 1:
            send_parts(0)
        points = xa[:, rows, :].reshape(PLANE * GROUP, features)
        norms = jnp.sum(points * points, axis=1, keepdims=True)
        cross = lax.dot_general(
            points, cc[...].reshape(2 * m, features), (((1,), (1,)), ((), ())),
            precision=HI, preferred_element_type=jnp.float32,
        )
        kernel = jnp.exp(-(norms + cn[0:1, :] - 2.0 * cross) / features)
        kk[:, rows, :] = kernel.reshape(PLANE, GROUP, 2 * m)
        part = jnp.dot(
            kernel, ww[...].reshape(2 * m, -1), precision=HI, preferred_element_type=jnp.float32
        )
        pp[:, rows, :] = part.reshape(PLANE, GROUP, -1)
    send_parts(1)

    cz = {}
    for g in range(2):
        rows = slice(g * GROUP, (g + 1) * GROUP)
        for q in range(1, PLANE):
            arrive(cp[g, opposite(q)])
        total = pp[0, rows, :]
        for q in range(1, PLANE):
            total = total + cb[q, rows, :]
        for k in range(rk):
            s3[rows, k, :] = total[:, k * lanes : (k + 1) * lanes]
        for d in far_first:
            s = (NEAR + d) % DEPTH
            if s // GROUP == g:
                cz[d] = remote(
                    s3.at[s], zb.at[(NEAR - d) % DEPTH], cz_s.at[d], cz_r.at[(NEAR - d) % DEPTH], z_peers[d]
                )
                go(cz[d])

    own = s3[NEAR]
    for s in range(DEPTH):
        if s != NEAR:
            landed_z(cz, s)
            own = own + zb[s]
    own = own * pred_scale
    for k in range(rk):
        piece = own[k : k + 1, :] - tg[:, k * lanes : (k + 1) * lanes]
        rz[NEAR, k : k + 1, :] = piece
        res_ref[:, k * lanes : (k + 1) * lanes] = piece

    dz = {
        d: remote(
            rz.at[NEAR], rz.at[(NEAR - d) % DEPTH], dz_s.at[d], dz_r.at[(NEAR - d) % DEPTH], z_peers[d]
        )
        for d in range(1, DEPTH)
    }
    for d in far_first:
        go(dz[d])

    dp = {}
    for g in range(2):
        rows = slice(g * GROUP, (g + 1) * GROUP)
        for s in range(g * GROUP, (g + 1) * GROUP):
            if s != NEAR:
                landed_z(dz, s)
        for k in range(rk):
            rb[0, rows, k * lanes : (k + 1) * lanes] = rz[rows, k, :]
        for q in plane_far_first:
            dp[g, q] = remote(
                rb.at[0, pl.ds(g * GROUP, GROUP)],
                rb.at[opposite(q), pl.ds(g * GROUP, GROUP)],
                dp_s.at[g, q], dp_r.at[g, opposite(q)], p_peers[q],
            )
            go(dp[g, q])

    change = None
    for g in range(2):
        rows = slice(g * GROUP, (g + 1) * GROUP)
        for q in range(1, PLANE):
            arrive(dp[g, opposite(q)])
        term = lax.dot_general(
            kk[:, rows, :].reshape(PLANE * GROUP, 2 * m),
            rb[:, rows, :].reshape(PLANE * GROUP, -1),
            (((0,), (0,)), ((), ())), precision=HI, preferred_element_type=jnp.float32,
        )
        change = term if change is None else change + term
    uu[...] = change
    swap_u = remote(uu.at[pl.ds(m, m)], ub, core_s.at[2], core_r.at[2], mate)
    go(swap_u)
    arrive(swap_u)
    new_ref[...] = ww[0] - step * (uu[0:m, :] + ub[...])

    for copy in sent:
        copy.wait_send()


def shards(batch, targets, centers, weights):
    m, features = centers.shape
    outputs = weights.shape[1]
    devices = lax.axis_size("wide") * lax.axis_size("narrow")
    all_rows = batch.shape[0] * lax.axis_size("wide")
    pred_scale = 8.0 / math.sqrt(m * devices)
    f32 = jnp.float32
    vmem = pltpu.VMEM
    dma = pltpu.SemaphoreType.DMA
    xk, rk = features // 128, outputs // 128
    scratch = [
        vmem(batch.shape, f32),
        vmem(targets.shape, f32),
        vmem((2, m, features), f32),
        vmem((2, m, outputs), f32),
        vmem((DEPTH, xk, 128), f32),
        vmem((PLANE, DEPTH, features), f32),
        vmem((8, 2 * m), f32),
        vmem((PLANE, DEPTH, 2 * m), f32),
        vmem((PLANE, DEPTH, outputs), f32),
        vmem((PLANE, DEPTH, outputs), f32),
        vmem((DEPTH, rk, 128), f32),
        vmem((DEPTH, rk, 128), f32),
        vmem((DEPTH, rk, 128), f32),
        vmem((PLANE, DEPTH, outputs), f32),
        vmem((2 * m, outputs), f32),
        vmem((m, outputs), f32),
        dma((4,)),
        dma((3,)), dma((3,)),
        dma((DEPTH,)), dma((DEPTH,)),
        dma((2, PLANE)), dma((2, PLANE)),
        dma((2, PLANE)), dma((2, PLANE)),
        dma((DEPTH,)), dma((DEPTH,)),
        dma((DEPTH,)), dma((DEPTH,)),
        dma((2, PLANE)), dma((2, PLANE)),
    ]
    return pl.pallas_call(
        functools.partial(body, pred_scale, 32.0 / all_rows),
        out_shape=(
            jax.ShapeDtypeStruct(targets.shape, f32),
            jax.ShapeDtypeStruct(weights.shape, f32),
        ),
        in_specs=[pl.BlockSpec(memory_space=pltpu.HBM)] * 4,
        out_specs=(pl.BlockSpec(memory_space=pltpu.VMEM),) * 2,
        scratch_shapes=scratch,
        compiler_params=pltpu.CompilerParams(
            collective_id=0, has_side_effects=True, vmem_limit_bytes=(64 << 20) - (160 << 10)
        ),
    )(batch, targets, centers, weights)


def solution(mesh):
    both = P(("wide", "narrow"), None)
    return jax.shard_map(
        shards, mesh=mesh, in_specs=(P("wide", None), both, both, both), out_specs=(both, both), check_vma=False
    )
```

```python
import functools
import math

import jax
import jax.numpy as jnp
from jax import lax
from jax.experimental import pallas as pl
from jax.experimental.pallas import tpu as pltpu
from jax.sharding import PartitionSpec as P

SIDE, DEPTH, CORES = 4, 16, 2
PLANE = SIDE * SIDE
GROUP = 8
REACH = 4
NEAR = 4
MESH = pl.DeviceIdType.MESH
HI = lax.Precision.HIGHEST


def place():
    w, n = lax.axis_index("wide"), lax.axis_index("narrow")
    core, rest = lax.rem(n, CORES), lax.div(n, CORES)
    x_lo, z = lax.div(w, DEPTH), lax.rem(w, DEPTH)
    x_hi, y = lax.rem(rest, 2), lax.div(rest, 2)
    return x_hi * 2 + x_lo, y, z, core, n


def name_of(x, y, z, core):
    return (lax.rem(x, 2) * DEPTH + z, (y * 2 + lax.div(x, 2)) * CORES + core)


def halves(v):
    top = v.astype(jnp.bfloat16)
    return top, (v - top.astype(jnp.float32)).astype(jnp.bfloat16)


def product(a, b, dims, last):
    def dot(u, v):
        return lax.dot_general(u, v, (dims, ((), ())), preferred_element_type=jnp.float32)

    low = dot(a[0], b[1]) + dot(a[1], b[0])
    if last:
        low = low + dot(a[1], b[1])
    return dot(a[0], b[0]) + low


def hops(d):
    return min(d, SIDE - d)


def body(
    pred_scale, step, batch_ref, targets_ref, centers_ref, weights_ref, res_ref, new_ref,
    xb, tg, cc, ww, ch, wh, z1, xa, cn, kt, pp, cb, s3, zb, rz, rb, uu, ub,
    lsem, core_s, core_r, az_s, az_r, ap_s, ap_r, cp_s, cp_r, cz_s, cz_r, dz_s, dz_r, dp_s, dp_r,
):
    x, y, z, core, n = place()
    features = cc.shape[2]
    m = cc.shape[1]
    lanes = 128
    xk = features // lanes
    rk = rb.shape[2] // lanes

    loads = [
        pltpu.make_async_copy(batch_ref, xb, lsem.at[0]),
        pltpu.make_async_copy(targets_ref, tg, lsem.at[1]),
        pltpu.make_async_copy(centers_ref, cc.at[0], lsem.at[2]),
        pltpu.make_async_copy(weights_ref, ww.at[0], lsem.at[3]),
    ]
    for load in loads:
        load.start()

    mate = name_of(x, y, z, 1 - core)
    z_peers = {d: name_of(x, y, lax.rem(z + d, DEPTH), core) for d in range(1, DEPTH)}
    p_peers = {
        q: name_of(lax.rem(x + q // SIDE, SIDE), lax.rem(y + q % SIDE, SIDE), z, core)
        for q in range(1, PLANE)
    }
    greeted = [mate, *p_peers.values()]
    greeted += [z_peers[d % DEPTH] for d in range(-REACH, REACH + 1) if d]
    barrier = pltpu.get_barrier_semaphore()
    for peer in greeted:
        pl.semaphore_signal(barrier, inc=1, device_id=peer, device_id_type=MESH)

    def remote(src, dst, send, recv, peer):
        return pltpu.make_async_remote_copy(
            src_ref=src, dst_ref=dst, send_sem=send, recv_sem=recv,
            device_id=peer, device_id_type=MESH,
        )

    sent = []

    def go(copy):
        copy.start()
        sent.append(copy)

    def arrive(copy):
        copy.wait_recv()

    def got(copy):
        copy.wait()

    def opposite(q):
        return (-(q // SIDE)) % SIDE * SIDE + (-(q % SIDE)) % SIDE

    far_first = sorted(range(1, DEPTH), key=lambda d: -min(d, DEPTH - d))
    plane_far_first = sorted(range(1, PLANE), key=lambda q: -hops(q // SIDE) - hops(q % SIDE))

    got(loads[0])
    mine = xb[pl.ds(n, 1), :]
    for k in range(xk):
        z1[NEAR, k : k + 1, :] = mine[:, k * lanes : (k + 1) * lanes]
    pl.semaphore_wait(barrier, len(greeted))

    az = {}

    def along_z(source, d, slot):
        az[slot] = remote(z1.at[source], z1.at[slot], az_s.at[slot], az_r.at[slot], z_peers[d % DEPTH])
        go(az[slot])

    for d in (4, -4, 3, -3, 2, -2, 1, -1):
        along_z(NEAR, d, NEAR - d)
    got(loads[2])
    swap_c = remote(cc.at[0], cc.at[1], core_s.at[0], core_r.at[0], mate)
    go(swap_c)
    got(loads[3])
    swap_w = remote(ww.at[0], ww.at[1], core_s.at[1], core_r.at[1], mate)
    go(swap_w)
    for s in (3, 5, 2, 6, 1, 7, 0):
        arrive(az[s])
        if s < NEAR:
            along_z(s, REACH, s + 12)
        else:
            along_z(s, -REACH, s + 4)

    ap = {}
    for g in range(2):
        rows = slice(g * GROUP, (g + 1) * GROUP)
        if g == 1:
            for s in range(GROUP, DEPTH):
                arrive(az[s])
        for k in range(xk):
            xa[0, rows, k * lanes : (k + 1) * lanes] = z1[rows, k, :]
        for q in plane_far_first:
            ap[g, q] = remote(
                xa.at[0, pl.ds(g * GROUP, GROUP)],
                xa.at[opposite(q), pl.ds(g * GROUP, GROUP)],
                ap_s.at[g, q], ap_r.at[g, opposite(q)], p_peers[q],
            )
            go(ap[g, q])

    def landed_z(copies, s):
        arrive(copies[(NEAR - s) % DEPTH])

    got(loads[1])
    arrive(swap_c)
    both = cc[...].reshape(2 * m, features)
    ones = jnp.ones((8, features), jnp.float32)
    cn[...] = lax.dot_general(
        ones, both * both, (((1,), (1,)), ((), ())), precision=HI, preferred_element_type=jnp.float32
    )
    ch[0], ch[1] = halves(both)
    arrive(swap_w)
    wh[0], wh[1] = halves(ww[...].reshape(2 * m, -1))

    cp = {}
    kernels = []

    def send_parts(g):
        for q in plane_far_first:
            cp[g, q] = remote(
                pp.at[q, pl.ds(g * GROUP, GROUP)],
                cb.at[opposite(q), pl.ds(g * GROUP, GROUP)],
                cp_s.at[g, q], cp_r.at[g, opposite(q)], p_peers[q],
            )
            go(cp[g, q])

    for g in range(2):
        rows = slice(g * GROUP, (g + 1) * GROUP)
        for q in range(1, PLANE):
            arrive(ap[g, opposite(q)])
        if g == 1:
            send_parts(0)
        points = xa[:, rows, :].reshape(PLANE * GROUP, features)
        norms = jnp.sum(points * points, axis=1, keepdims=True)
        cross = product(halves(points), (ch[0], ch[1]), ((1,), (1,)), True)
        kernel = jnp.exp(-(norms + cn[0:1, :] - 2.0 * cross) / features)
        kernel_halves = halves(kernel)
        part = product(kernel_halves, (wh[0], wh[1]), ((1,), (0,)), False)
        pp[:, rows, :] = part.reshape(PLANE, GROUP, -1)
        kernels.append(kernel)
    send_parts(1)
    for g in range(2):
        kt[g, 0], kt[g, 1] = halves(kernels[g].T)

    cz = {}
    for g in range(2):
        rows = slice(g * GROUP, (g + 1) * GROUP)
        for q in range(1, PLANE):
            arrive(cp[g, opposite(q)])
        total = pp[0, rows, :]
        for q in range(1, PLANE):
            total = total + cb[q, rows, :]
        for k in range(rk):
            s3[rows, k, :] = total[:, k * lanes : (k + 1) * lanes]
        for d in far_first:
            s = (NEAR + d) % DEPTH
            if s // GROUP == g:
                cz[d] = remote(
                    s3.at[s], zb.at[(NEAR - d) % DEPTH], cz_s.at[d], cz_r.at[(NEAR - d) % DEPTH], z_peers[d]
                )
                go(cz[d])

    own = s3[NEAR]
    for s in range(DEPTH):
        if s != NEAR:
            landed_z(cz, s)
            own = own + zb[s]
    own = own * pred_scale
    for k in range(rk):
        piece = own[k : k + 1, :] - tg[:, k * lanes : (k + 1) * lanes]
        rz[NEAR, k : k + 1, :] = piece
        res_ref[:, k * lanes : (k + 1) * lanes] = piece

    dz = {
        d: remote(
            rz.at[NEAR], rz.at[(NEAR - d) % DEPTH], dz_s.at[d], dz_r.at[(NEAR - d) % DEPTH], z_peers[d]
        )
        for d in range(1, DEPTH)
    }
    for d in far_first:
        go(dz[d])

    dp = {}
    for g in range(2):
        rows = slice(g * GROUP, (g + 1) * GROUP)
        for s in range(g * GROUP, (g + 1) * GROUP):
            if s != NEAR:
                landed_z(dz, s)
        for k in range(rk):
            rb[0, rows, k * lanes : (k + 1) * lanes] = rz[rows, k, :]
        for q in plane_far_first:
            dp[g, q] = remote(
                rb.at[0, pl.ds(g * GROUP, GROUP)],
                rb.at[opposite(q), pl.ds(g * GROUP, GROUP)],
                dp_s.at[g, q], dp_r.at[g, opposite(q)], p_peers[q],
            )
            go(dp[g, q])

    change = None
    for g in range(2):
        rows = slice(g * GROUP, (g + 1) * GROUP)
        for q in range(1, PLANE):
            arrive(dp[g, opposite(q)])
        term = product(
            (kt[g, 0], kt[g, 1]), halves(rb[:, rows, :].reshape(PLANE * GROUP, -1)), ((1,), (0,)), False
        )
        change = term if change is None else change + term
    uu[...] = change
    swap_u = remote(uu.at[pl.ds(m, m)], ub, core_s.at[2], core_r.at[2], mate)
    go(swap_u)
    arrive(swap_u)
    new_ref[...] = ww[0] - step * (uu[0:m, :] + ub[...])

    for copy in sent:
        copy.wait_send()


def shards(batch, targets, centers, weights):
    m, features = centers.shape
    outputs = weights.shape[1]
    devices = lax.axis_size("wide") * lax.axis_size("narrow")
    all_rows = batch.shape[0] * lax.axis_size("wide")
    pred_scale = 8.0 / math.sqrt(m * devices)
    f32, bf16 = jnp.float32, jnp.bfloat16
    vmem = pltpu.VMEM
    dma = pltpu.SemaphoreType.DMA
    xk, rk = features // 128, outputs // 128
    scratch = [
        vmem(batch.shape, f32),
        vmem(targets.shape, f32),
        vmem((2, m, features), f32),
        vmem((2, m, outputs), f32),
        vmem((2, 2 * m, features), bf16),
        vmem((2, 2 * m, outputs), bf16),
        vmem((DEPTH, xk, 128), f32),
        vmem((PLANE, DEPTH, features), f32),
        vmem((8, 2 * m), f32),
        vmem((2, 2, 2 * m, PLANE * GROUP), bf16),
        vmem((PLANE, DEPTH, outputs), f32),
        vmem((PLANE, DEPTH, outputs), f32),
        vmem((DEPTH, rk, 128), f32),
        vmem((DEPTH, rk, 128), f32),
        vmem((DEPTH, rk, 128), f32),
        vmem((PLANE, DEPTH, outputs), f32),
        vmem((2 * m, outputs), f32),
        vmem((m, outputs), f32),
        dma((4,)),
        dma((3,)), dma((3,)),
        dma((DEPTH,)), dma((DEPTH,)),
        dma((2, PLANE)), dma((2, PLANE)),
        dma((2, PLANE)), dma((2, PLANE)),
        dma((DEPTH,)), dma((DEPTH,)),
        dma((DEPTH,)), dma((DEPTH,)),
        dma((2, PLANE)), dma((2, PLANE)),
    ]
    return pl.pallas_call(
        functools.partial(body, pred_scale, 32.0 / all_rows),
        out_shape=(
            jax.ShapeDtypeStruct(targets.shape, f32),
            jax.ShapeDtypeStruct(weights.shape, f32),
        ),
        in_specs=[pl.BlockSpec(memory_space=pltpu.HBM)] * 4,
        out_specs=(pl.BlockSpec(memory_space=pltpu.VMEM),) * 2,
        scratch_shapes=scratch,
        compiler_params=pltpu.CompilerParams(
            collective_id=0, has_side_effects=True, vmem_limit_bytes=48 << 20
        ),
    )(*(pltpu.with_memory_space_constraint(a, pltpu.HBM) for a in (batch, targets, centers, weights)))


def solution(mesh):
    both = P(("wide", "narrow"), None)
    return jax.shard_map(
        shards, mesh=mesh, in_specs=(P("wide", None), both, both, both), out_specs=(both, both), check_vma=False
    )
```

```python
import functools
import math

import jax
import jax.numpy as jnp
from jax import lax
from jax.experimental import pallas as pl
from jax.experimental.pallas import tpu as pltpu
from jax.sharding import PartitionSpec as P

SIDE, DEPTH, CORES = 4, 16, 2
PLANE = SIDE * SIDE
GROUP = 8
REACH = 4
SPREAD = (0, 1, -1, 2)
PIECES = ((0, 1), (1, 2), (3, 1))
NEAR = 4
MESH = pl.DeviceIdType.MESH
HI = lax.Precision.HIGHEST


def place():
    w, n = lax.axis_index("wide"), lax.axis_index("narrow")
    core, rest = lax.rem(n, CORES), lax.div(n, CORES)
    x_lo, z = lax.div(w, DEPTH), lax.rem(w, DEPTH)
    x_hi, y = lax.rem(rest, 2), lax.div(rest, 2)
    return x_hi * 2 + x_lo, y, z, core, n


def name_of(x, y, z, core):
    return (lax.rem(x, 2) * DEPTH + z, (y * 2 + lax.div(x, 2)) * CORES + core)


def halves(v):
    top = v.astype(jnp.bfloat16)
    return top, (v - top.astype(jnp.float32)).astype(jnp.bfloat16)


def product(a, b, dims, last):
    def dot(u, v):
        return lax.dot_general(u, v, (dims, ((), ())), preferred_element_type=jnp.float32)

    low = dot(a[0], b[1]) + dot(a[1], b[0])
    if last:
        low = low + dot(a[1], b[1])
    return dot(a[0], b[0]) + low


def hops(d):
    return min(d, SIDE - d)


def body(
    pred_scale, step, batch_ref, targets_ref, centers_ref, weights_ref, res_ref, new_ref,
    xb, tg, cc, ww, ch, wh, z1, xa, cn, kt, pp, cb, s3, t4, s4, nb, ft, fb, rb, uu, ub,
    lsem, core_s, core_r, az_s, az_r, ap_s, ap_r, cp_s, cp_r, nz_s, nz_r, fz_s, fz_r, gz_s, gz_r, dp_s, dp_r,
):
    x, y, z, core, n = place()
    features = cc.shape[2]
    m = cc.shape[1]
    lanes = 128
    xk = features // lanes
    rk = rb.shape[2]

    loads = [
        pltpu.make_async_copy(batch_ref, xb, lsem.at[0]),
        pltpu.make_async_copy(targets_ref, tg, lsem.at[1]),
        pltpu.make_async_copy(centers_ref, cc.at[0], lsem.at[2]),
        pltpu.make_async_copy(weights_ref, ww.at[0], lsem.at[3]),
    ]
    for load in loads:
        load.start()

    mate = name_of(x, y, z, 1 - core)
    z_peers = {d: name_of(x, y, lax.rem(z + d, DEPTH), core) for d in range(1, DEPTH)}
    p_peers = {
        q: name_of(lax.rem(x + q // SIDE, SIDE), lax.rem(y + q % SIDE, SIDE), z, core)
        for q in range(1, PLANE)
    }
    greeted = [mate, *p_peers.values()]
    greeted += [z_peers[d % DEPTH] for d in range(-REACH, REACH + 1) if d]
    barrier = pltpu.get_barrier_semaphore()
    for peer in greeted:
        pl.semaphore_signal(barrier, inc=1, device_id=peer, device_id_type=MESH)

    def remote(src, dst, send, recv, peer):
        return pltpu.make_async_remote_copy(
            src_ref=src, dst_ref=dst, send_sem=send, recv_sem=recv,
            device_id=peer, device_id_type=MESH,
        )

    sent = []

    def go(copy):
        copy.start()
        sent.append(copy)

    def arrive(copy):
        copy.wait_recv()

    def got(copy):
        copy.wait()

    def opposite(q):
        return (-(q // SIDE)) % SIDE * SIDE + (-(q % SIDE)) % SIDE

    far_first = sorted(range(1, DEPTH), key=lambda d: -min(d, DEPTH - d))
    plane_far_first = sorted(range(1, PLANE), key=lambda q: -hops(q // SIDE) - hops(q % SIDE))

    got(loads[0])
    mine = xb[pl.ds(n, 1), :]
    for k in range(xk):
        z1[NEAR, k : k + 1, :] = mine[:, k * lanes : (k + 1) * lanes]
    pl.semaphore_wait(barrier, len(greeted))

    az = {}

    def along_z(source, d, slot):
        az[slot] = remote(z1.at[source], z1.at[slot], az_s.at[slot], az_r.at[slot], z_peers[d % DEPTH])
        go(az[slot])

    for d in (4, -4, 3, -3, 2, -2, 1, -1):
        along_z(NEAR, d, NEAR - d)
    got(loads[2])
    swap_c = remote(cc.at[0], cc.at[1], core_s.at[0], core_r.at[0], mate)
    go(swap_c)
    got(loads[3])
    swap_w = remote(ww.at[0], ww.at[1], core_s.at[1], core_r.at[1], mate)
    go(swap_w)
    for s in (3, 5, 2, 6, 1, 7, 0):
        arrive(az[s])
        if s < NEAR:
            along_z(s, REACH, s + 12)
        else:
            along_z(s, -REACH, s + 4)

    ap = {}
    for g in range(2):
        rows = slice(g * GROUP, (g + 1) * GROUP)
        if g == 1:
            for s in range(GROUP, DEPTH):
                arrive(az[s])
        for k in range(xk):
            xa[0, rows, k * lanes : (k + 1) * lanes] = z1[rows, k, :]
        for q in plane_far_first:
            ap[g, q] = remote(
                xa.at[0, pl.ds(g * GROUP, GROUP)],
                xa.at[opposite(q), pl.ds(g * GROUP, GROUP)],
                ap_s.at[g, q], ap_r.at[g, opposite(q)], p_peers[q],
            )
            go(ap[g, q])

    got(loads[1])
    arrive(swap_c)
    both = cc[...].reshape(2 * m, features)
    ones = jnp.ones((8, features), jnp.float32)
    cn[...] = lax.dot_general(
        ones, both * both, (((1,), (1,)), ((), ())), precision=HI, preferred_element_type=jnp.float32
    )
    ch[0], ch[1] = halves(both)
    arrive(swap_w)
    wh[0], wh[1] = halves(ww[...].reshape(2 * m, -1))

    cp = {}
    kernels = []

    def send_parts(g):
        for q in plane_far_first:
            cp[g, q] = remote(
                pp.at[q, pl.ds(g * GROUP, GROUP)],
                cb.at[opposite(q), pl.ds(g * GROUP, GROUP)],
                cp_s.at[g, q], cp_r.at[g, opposite(q)], p_peers[q],
            )
            go(cp[g, q])

    for g in range(2):
        rows = slice(g * GROUP, (g + 1) * GROUP)
        for q in range(1, PLANE):
            arrive(ap[g, opposite(q)])
        if g == 1:
            send_parts(0)
        points = xa[:, rows, :].reshape(PLANE * GROUP, features)
        norms = jnp.sum(points * points, axis=1, keepdims=True)
        cross = product(halves(points), (ch[0], ch[1]), ((1,), (1,)), True)
        kernel = jnp.exp(-(norms + cn[0:1, :] - 2.0 * cross) / features)
        kernel_halves = halves(kernel)
        part = product(kernel_halves, (wh[0], wh[1]), ((1,), (0,)), False)
        pp[:, rows, :] = part.reshape(PLANE, GROUP, -1)
        kernels.append(kernel_halves)
    send_parts(1)

    wide_shape = (PLANE * GROUP, PLANE * DEPTH)
    row, col = (lax.broadcasted_iota(jnp.int32, wide_shape, axis) for axis in (0, 1))
    block, step4 = col // (PLANE * 4), col % 4
    shift = jnp.zeros_like(col)
    for b in range(1, 4):
        shift = jnp.where(block == b, SPREAD[b], shift)
    wanted = (4 * step4 - shift + DEPTH) % DEPTH
    same_plane = row // GROUP == col % (PLANE * 4) // 4
    for half in range(2):
        turned = None
        for g in range(2):
            pick = jnp.where(same_plane & (wanted == row % GROUP + g * GROUP), 1.0, 0.0).astype(jnp.bfloat16)
            term = lax.dot_general(
                kernels[g][half], pick, (((0,), (0,)), ((), ())), preferred_element_type=jnp.float32
            )
            turned = term if turned is None else turned + term
        kt[half] = turned.astype(jnp.bfloat16)

    for k in range(rk):
        t4[k : k + 1, :] = tg[:, k * lanes : (k + 1) * lanes]
    for g in range(2):
        rows = slice(g * GROUP, (g + 1) * GROUP)
        for q in range(1, PLANE):
            arrive(cp[g, opposite(q)])
        total = pp[0, rows, :]
        for q in range(1, PLANE):
            total = total + cb[q, rows, :]
        for k in range(rk):
            s3[rows, k, :] = total[:, k * lanes : (k + 1) * lanes]
        for s in range(g * GROUP, (g + 1) * GROUP):
            scaled = s3[s] * pred_scale
            s4[s % 4, s // 4] = scaled - t4[...] if s == NEAR else scaled

    nz = {}
    for j, e in ((2, -2), (0, 1), (1, -1)):
        nz[j] = remote(s4.at[e % 4], nb.at[j], nz_s.at[j], nz_r.at[j], z_peers[e % DEPTH])
        go(nz[j])
    for j in (0, 1, 2):
        arrive(nz[j])
    for i in range(4):
        ft[i] = s4[0, i] + nb[0, i] + nb[1, (i - 1) % 4] + nb[2, (i - 1) % 4]
    fz = {}
    for j in (2, 1, 3):
        fz[j] = remote(ft, fb.at[j], fz_s.at[j], fz_r.at[j], z_peers[DEPTH - 4 * j])
        go(fz[j])
    for j in (1, 3, 2):
        arrive(fz[j])
    for i in range(4):
        rb[0, i] = ft[i] + fb[1, (i - 1) % 4] + fb[2, (i - 2) % 4] + fb[3, (i - 3) % 4]

    gz = {}
    for b in (3, 1, 2):
        gz[b] = remote(
            rb.at[0, pl.ds(0, 4)], rb.at[b, pl.ds(0, 4)], gz_s.at[b], gz_r.at[b], z_peers[SPREAD[b] % DEPTH]
        )
        go(gz[b])
    dp = {}
    for p, (first, count) in enumerate(PIECES):
        for b in range(first, first + count):
            if b:
                arrive(gz[b])
        for q in plane_far_first:
            dp[p, q] = remote(
                rb.at[pl.ds(first, count), pl.ds(0, 4)],
                rb.at[pl.ds(first, count), pl.ds(opposite(q) * 4, 4)],
                dp_s.at[p, q], dp_r.at[p, opposite(q)], p_peers[q],
            )
            go(dp[p, q])
        if p == 0:
            for k in range(rk):
                res_ref[:, k * lanes : (k + 1) * lanes] = rb[0, 1, k : k + 1, :]

    change = None
    for h in range(2):
        for p in ((0, 1), (2,))[h]:
            for q in range(1, PLANE):
                arrive(dp[p, opposite(q)])
        rows = jnp.concatenate(
            [rb[2 * h : 2 * h + 2, :, k, :].reshape(PLANE * GROUP, lanes) for k in range(rk)], axis=1
        )
        columns = slice(h * PLANE * GROUP, (h + 1) * PLANE * GROUP)
        term = product((kt[0, :, columns], kt[1, :, columns]), halves(rows), ((1,), (0,)), False)
        change = term if change is None else change + term
    uu[...] = change
    swap_u = remote(uu.at[pl.ds(m, m)], ub, core_s.at[2], core_r.at[2], mate)
    go(swap_u)
    arrive(swap_u)
    new_ref[...] = ww[0] - step * (uu[0:m, :] + ub[...])

    for copy in sent:
        copy.wait_send()


def shards(batch, targets, centers, weights):
    m, features = centers.shape
    outputs = weights.shape[1]
    devices = lax.axis_size("wide") * lax.axis_size("narrow")
    all_rows = batch.shape[0] * lax.axis_size("wide")
    pred_scale = 8.0 / math.sqrt(m * devices)
    f32, bf16 = jnp.float32, jnp.bfloat16
    vmem = pltpu.VMEM
    dma = pltpu.SemaphoreType.DMA
    xk, rk = features // 128, outputs // 128
    scratch = [
        vmem(batch.shape, f32),
        vmem(targets.shape, f32),
        vmem((2, m, features), f32),
        vmem((2, m, outputs), f32),
        vmem((2, 2 * m, features), bf16),
        vmem((2, 2 * m, outputs), bf16),
        vmem((DEPTH, xk, 128), f32),
        vmem((PLANE, DEPTH, features), f32),
        vmem((8, 2 * m), f32),
        vmem((2, 2 * m, PLANE * DEPTH), bf16),
        vmem((PLANE, DEPTH, outputs), f32),
        vmem((PLANE, DEPTH, outputs), f32),
        vmem((DEPTH, rk, 128), f32),
        vmem((rk, 128), f32),
        vmem((4, 4, rk, 128), f32),
        vmem((3, 4, rk, 128), f32),
        vmem((4, rk, 128), f32),
        vmem((4, 4, rk, 128), f32),
        vmem((4, PLANE * 4, rk, 128), f32),
        vmem((2 * m, outputs), f32),
        vmem((m, outputs), f32),
        dma((4,)),
        dma((3,)), dma((3,)),
        dma((DEPTH,)), dma((DEPTH,)),
        dma((2, PLANE)), dma((2, PLANE)),
        dma((2, PLANE)), dma((2, PLANE)),
        dma((3,)), dma((3,)),
        dma((4,)), dma((4,)),
        dma((4,)), dma((4,)),
        dma((len(PIECES), PLANE)), dma((len(PIECES), PLANE)),
    ]
    return pl.pallas_call(
        functools.partial(body, pred_scale, 32.0 / all_rows),
        out_shape=(
            jax.ShapeDtypeStruct(targets.shape, f32),
            jax.ShapeDtypeStruct(weights.shape, f32),
        ),
        in_specs=[pl.BlockSpec(memory_space=pltpu.HBM)] * 4,
        out_specs=(pl.BlockSpec(memory_space=pltpu.VMEM),) * 2,
        scratch_shapes=scratch,
        compiler_params=pltpu.CompilerParams(
            collective_id=0, has_side_effects=True, vmem_limit_bytes=48 << 20
        ),
    )(*(pltpu.with_memory_space_constraint(a, pltpu.HBM) for a in (batch, targets, centers, weights)))


def solution(mesh):
    both = P(("wide", "narrow"), None)
    return jax.shard_map(
        shards, mesh=mesh, in_specs=(P("wide", None), both, both, both), out_specs=(both, both), check_vma=False
    )
```

```python
import functools
import math

import jax
import jax.numpy as jnp
from jax import lax
from jax.experimental import pallas as pl
from jax.experimental.pallas import tpu as pltpu
from jax.sharding import PartitionSpec as P

SIDE, DEPTH, CORES = 4, 16, 2
PLANE = SIDE * SIDE
GROUP = 8
REACH = 4
NEAR = 4
MESH = pl.DeviceIdType.MESH
HI = lax.Precision.HIGHEST


def place():
    w, n = lax.axis_index("wide"), lax.axis_index("narrow")
    core, rest = lax.rem(n, CORES), lax.div(n, CORES)
    x_lo, z = lax.div(w, DEPTH), lax.rem(w, DEPTH)
    x_hi, y = lax.rem(rest, 2), lax.div(rest, 2)
    return x_hi * 2 + x_lo, y, z, core, n


def name_of(x, y, z, core):
    return (lax.rem(x, 2) * DEPTH + z, (y * 2 + lax.div(x, 2)) * CORES + core)


def halves(v):
    top = v.astype(jnp.bfloat16)
    return top, (v - top.astype(jnp.float32)).astype(jnp.bfloat16)


def product(a, b, dims, last):
    def dot(u, v):
        return lax.dot_general(u, v, (dims, ((), ())), preferred_element_type=jnp.float32)

    low = dot(a[0], b[1]) + dot(a[1], b[0])
    if last:
        low = low + dot(a[1], b[1])
    return dot(a[0], b[0]) + low


def hops(d):
    return min(d, SIDE - d)


def body(
    pred_scale, step, batch_ref, targets_ref, centers_ref, weights_ref, res_ref, new_ref,
    xb, tg, cc, ww, ch, wh, z1, xa, cn, kt, pp, cb, s3, zb, rz, rb, uu, ub,
    lsem, core_s, core_r, az_s, az_r, ap_s, ap_r, cp_s, cp_r, cz_s, cz_r, dz_s, dz_r, dp_s, dp_r,
):
    x, y, z, core, n = place()
    features = cc.shape[2]
    m = cc.shape[1]
    lanes = 128
    xk = features // lanes
    rk = rb.shape[2] // lanes

    loads = [
        pltpu.make_async_copy(batch_ref, xb, lsem.at[0]),
        pltpu.make_async_copy(targets_ref, tg, lsem.at[1]),
        pltpu.make_async_copy(centers_ref, cc.at[0], lsem.at[2]),
        pltpu.make_async_copy(weights_ref, ww.at[0], lsem.at[3]),
    ]
    for load in loads:
        load.start()

    def around(at, size):
        return [at] + [jnp.where(at + d >= size, at + d - size, at + d) for d in range(1, size)]

    zs, xs, ys = around(z, DEPTH), around(x, SIDE), around(y, SIDE)
    here = lax.axis_index("wide") - z
    x_low = [lax.rem(v, 2) * DEPTH + z for v in xs]
    x_high = [lax.div(v, 2) * CORES + core for v in xs]
    y_high = [v * (2 * CORES) for v in ys]
    mate = (here + z, n + 1 - 2 * core)
    z_peers = {d: (here + zs[d], n) for d in range(1, DEPTH)}
    p_peers = {
        q: (x_low[q // SIDE], x_high[q // SIDE] + y_high[q % SIDE]) for q in range(1, PLANE)
    }
    greeted = [mate, *p_peers.values()]
    greeted += [z_peers[d % DEPTH] for d in range(-REACH, REACH + 1) if d]
    barrier = pltpu.get_barrier_semaphore()
    for peer in greeted:
        pl.semaphore_signal(barrier, inc=1, device_id=peer, device_id_type=MESH)

    def remote(src, dst, send, recv, peer):
        return pltpu.make_async_remote_copy(
            src_ref=src, dst_ref=dst, send_sem=send, recv_sem=recv,
            device_id=peer, device_id_type=MESH,
        )

    def all_in(buffer, sem):
        remote(buffer, buffer, sem, sem, mate).wait_recv()

    def all_out(buffer, sem):
        remote(buffer, buffer, sem, sem, mate).wait_send()

    def opposite(q):
        return (-(q // SIDE)) % SIDE * SIDE + (-(q % SIDE)) % SIDE

    far_first = sorted(range(1, DEPTH), key=lambda d: -min(d, DEPTH - d))
    plane_far_first = sorted(range(1, PLANE), key=lambda q: -hops(q // SIDE) - hops(q % SIDE))

    loads[0].wait()
    mine = xb[pl.ds(n, 1), :]
    for k in range(xk):
        z1[NEAR, k : k + 1, :] = mine[:, k * lanes : (k + 1) * lanes]
    pl.semaphore_wait(barrier, len(greeted))

    def along_z(first, count, d, there, part):
        remote(
            z1.at[pl.ds(first, count)], z1.at[pl.ds(there, count)], az_s.at[0], az_r.at[part], z_peers[d % DEPTH]
        ).start()

    for d in (4, -4, 3, -3, 2, -2, 1, -1):
        slot = NEAR - d
        along_z(NEAR, 1, d, slot, 0 if slot < NEAR else 1 if slot < GROUP else 2)
    loads[2].wait()
    swap_c = remote(cc.at[0], cc.at[1], core_s.at[0], core_r.at[0], mate)
    swap_c.start()
    loads[3].wait()
    swap_w = remote(ww.at[0], ww.at[1], core_s.at[1], core_r.at[1], mate)
    swap_w.start()
    all_in(z1.at[pl.ds(0, 4)], az_r.at[0])
    along_z(0, 4, REACH, 12, 2)
    all_in(z1.at[pl.ds(5, 3)], az_r.at[1])
    along_z(5, 3, -REACH, 9, 2)

    for g in range(2):
        rows = slice(g * GROUP, (g + 1) * GROUP)
        here = pl.ds(g * GROUP, GROUP)
        if g == 1:
            all_in(z1.at[here], az_r.at[2])
        for k in range(xk):
            xa[0, rows, k * lanes : (k + 1) * lanes] = z1[rows, k, :]
        for q in plane_far_first:
            remote(xa.at[0, here], xa.at[opposite(q), here], ap_s.at[0], ap_r.at[g], p_peers[q]).start()

    loads[1].wait()
    swap_c.wait_recv()
    both = cc[...].reshape(2 * m, features)
    ones = jnp.ones((8, features), jnp.float32)
    cn[...] = lax.dot_general(
        ones, both * both, (((1,), (1,)), ((), ())), precision=HI, preferred_element_type=jnp.float32
    )
    ch[0], ch[1] = halves(both)
    swap_w.wait_recv()
    wh[0], wh[1] = halves(ww[...].reshape(2 * m, -1))

    kernels = []
    others = pl.ds(1, PLANE - 1)

    def send_parts(g):
        here = pl.ds(g * GROUP, GROUP)
        for q in plane_far_first:
            remote(pp.at[q, here], cb.at[opposite(q), here], cp_s.at[0], cp_r.at[g], p_peers[q]).start()

    for g in range(2):
        rows = slice(g * GROUP, (g + 1) * GROUP)
        all_in(xa.at[others, pl.ds(g * GROUP, GROUP)], ap_r.at[g])
        if g == 1:
            send_parts(0)
        points = xa[:, rows, :].reshape(PLANE * GROUP, features)
        norms = jnp.sum(points * points, axis=1, keepdims=True)
        cross = product(halves(points), (ch[0], ch[1]), ((1,), (1,)), True)
        kernel = jnp.exp(-(norms + cn[0:1, :] - 2.0 * cross) / features)
        kernel_halves = halves(kernel)
        part = product(kernel_halves, (wh[0], wh[1]), ((1,), (0,)), False)
        pp[:, rows, :] = part.reshape(PLANE, GROUP, -1)
        kernels.append(kernel)
    send_parts(1)
    for g in range(2):
        kt[g, 0], kt[g, 1] = halves(kernels[g].T)

    for g in range(2):
        rows = slice(g * GROUP, (g + 1) * GROUP)
        all_in(cb.at[others, pl.ds(g * GROUP, GROUP)], cp_r.at[g])
        total = pp[0, rows, :]
        for q in range(1, PLANE):
            total = total + cb[q, rows, :]
        for k in range(rk):
            s3[rows, k, :] = total[:, k * lanes : (k + 1) * lanes]
        for d in far_first:
            s = (NEAR + d) % DEPTH
            if s // GROUP == g:
                remote(s3.at[s], zb.at[DEPTH - 1 - d], cz_s.at[0], cz_r.at[0], z_peers[d]).start()

    own = s3[NEAR]
    all_in(zb, cz_r.at[0])
    for s in range(DEPTH - 1):
        own = own + zb[s]
    own = own * pred_scale
    for k in range(rk):
        piece = own[k : k + 1, :] - tg[:, k * lanes : (k + 1) * lanes]
        rz[NEAR, k : k + 1, :] = piece
        res_ref[:, k * lanes : (k + 1) * lanes] = piece

    for d in far_first:
        slot = (NEAR - d) % DEPTH
        remote(rz.at[NEAR], rz.at[slot], dz_s.at[0], dz_r.at[slot // GROUP], z_peers[d]).start()

    for g in range(2):
        rows = slice(g * GROUP, (g + 1) * GROUP)
        here = pl.ds(g * GROUP, GROUP)
        all_in(rz.at[pl.ds(g * GROUP, GROUP - 1 + g)], dz_r.at[g])
        for k in range(rk):
            rb[0, rows, k * lanes : (k + 1) * lanes] = rz[rows, k, :]
        for q in plane_far_first:
            remote(rb.at[0, here], rb.at[opposite(q), here], dp_s.at[0], dp_r.at[g], p_peers[q]).start()

    change = None
    for g in range(2):
        rows = slice(g * GROUP, (g + 1) * GROUP)
        all_in(rb.at[others, pl.ds(g * GROUP, GROUP)], dp_r.at[g])
        term = product(
            (kt[g, 0], kt[g, 1]), halves(rb[:, rows, :].reshape(PLANE * GROUP, -1)), ((1,), (0,)), False
        )
        change = term if change is None else change + term
    uu[...] = change
    swap_u = remote(uu.at[pl.ds(m, m)], ub, core_s.at[2], core_r.at[2], mate)
    swap_u.start()
    swap_u.wait_recv()
    new_ref[...] = ww[0] - step * (uu[0:m, :] + ub[...])

    for swap in (swap_c, swap_w, swap_u):
        swap.wait_send()
    all_out(z1.at[pl.ds(0, DEPTH - 1)], az_s.at[0])
    all_out(xa.at[others], ap_s.at[0])
    all_out(pp.at[others], cp_s.at[0])
    all_out(zb, cz_s.at[0])
    all_out(rz.at[pl.ds(0, DEPTH - 1)], dz_s.at[0])
    all_out(rb.at[others], dp_s.at[0])


def shards(batch, targets, centers, weights):
    m, features = centers.shape
    outputs = weights.shape[1]
    devices = lax.axis_size("wide") * lax.axis_size("narrow")
    all_rows = batch.shape[0] * lax.axis_size("wide")
    pred_scale = 8.0 / math.sqrt(m * devices)
    f32, bf16 = jnp.float32, jnp.bfloat16
    vmem = pltpu.VMEM
    dma = pltpu.SemaphoreType.DMA
    xk, rk = features // 128, outputs // 128
    scratch = [
        vmem(batch.shape, f32),
        vmem(targets.shape, f32),
        vmem((2, m, features), f32),
        vmem((2, m, outputs), f32),
        vmem((2, 2 * m, features), bf16),
        vmem((2, 2 * m, outputs), bf16),
        vmem((DEPTH, xk, 128), f32),
        vmem((PLANE, DEPTH, features), f32),
        vmem((8, 2 * m), f32),
        vmem((2, 2, 2 * m, PLANE * GROUP), bf16),
        vmem((PLANE, DEPTH, outputs), f32),
        vmem((PLANE, DEPTH, outputs), f32),
        vmem((DEPTH, rk, 128), f32),
        vmem((DEPTH - 1, rk, 128), f32),
        vmem((DEPTH, rk, 128), f32),
        vmem((PLANE, DEPTH, outputs), f32),
        vmem((2 * m, outputs), f32),
        vmem((m, outputs), f32),
        dma((4,)),
        dma((3,)), dma((3,)),
        dma((1,)), dma((3,)),
        dma((1,)), dma((2,)),
        dma((1,)), dma((2,)),
        dma((1,)), dma((1,)),
        dma((1,)), dma((2,)),
        dma((1,)), dma((2,)),
    ]
    return pl.pallas_call(
        functools.partial(body, pred_scale, 32.0 / all_rows),
        out_shape=(
            jax.ShapeDtypeStruct(targets.shape, f32),
            jax.ShapeDtypeStruct(weights.shape, f32),
        ),
        in_specs=[pl.BlockSpec(memory_space=pltpu.HBM)] * 4,
        out_specs=(pl.BlockSpec(memory_space=pltpu.VMEM),) * 2,
        scratch_shapes=scratch,
        compiler_params=pltpu.CompilerParams(
            collective_id=0, has_side_effects=True, vmem_limit_bytes=48 << 20
        ),
    )(*(pltpu.with_memory_space_constraint(a, pltpu.HBM) for a in (batch, targets, centers, weights)))


def solution(mesh):
    both = P(("wide", "narrow"), None)
    return jax.shard_map(
        shards, mesh=mesh, in_specs=(P("wide", None), both, both, both), out_specs=(both, both), check_vma=False
    )
```

```python
import functools
import math

import jax
import jax.numpy as jnp
from jax import lax
from jax.experimental import pallas as pl
from jax.experimental.pallas import tpu as pltpu
from jax.sharding import PartitionSpec as P

SIDE, DEPTH, CORES = 4, 16, 2
PLANE = SIDE * SIDE
GROUP = 8
REACH = 4
NEAR = 4
MESH = pl.DeviceIdType.MESH
HI = lax.Precision.HIGHEST


def place():
    w, n = lax.axis_index("wide"), lax.axis_index("narrow")
    core, rest = lax.rem(n, CORES), lax.div(n, CORES)
    x_lo, z = lax.div(w, DEPTH), lax.rem(w, DEPTH)
    x_hi, y = lax.rem(rest, 2), lax.div(rest, 2)
    return x_hi * 2 + x_lo, y, z, core, n


def name_of(x, y, z, core):
    return (lax.rem(x, 2) * DEPTH + z, (y * 2 + lax.div(x, 2)) * CORES + core)


def halves(v):
    top = v.astype(jnp.bfloat16)
    return top, (v - top.astype(jnp.float32)).astype(jnp.bfloat16)


def product(a, b, dims, last):
    def dot(u, v):
        return lax.dot_general(u, v, (dims, ((), ())), preferred_element_type=jnp.float32)

    low = dot(a[0], b[1]) + dot(a[1], b[0])
    if last:
        low = low + dot(a[1], b[1])
    return dot(a[0], b[0]) + low


def hops(d):
    return min(d, SIDE - d)


def body(
    pred_scale, step, batch_ref, targets_ref, centers_ref, weights_ref, res_ref, new_ref,
    xb, tg, cc, ww, ch, wh, z1, xa, cn, kt, pp, cb, s3, zb, rz, rb, uu, ub,
    lsem, core_s, core_r, az_s, az_r, ap_s, ap_r, cp_s, cp_r, cz_s, cz_r, dz_s, dz_r, dp_s, dp_r,
):
    x, y, z, core, n = place()
    features = cc.shape[2]
    m = cc.shape[1]
    lanes = 128
    xk = features // lanes
    rk = rb.shape[2] // lanes

    loads = [
        pltpu.make_async_copy(batch_ref, xb, lsem.at[0]),
        pltpu.make_async_copy(targets_ref, tg, lsem.at[1]),
        pltpu.make_async_copy(centers_ref, cc.at[0], lsem.at[2]),
        pltpu.make_async_copy(weights_ref, ww.at[0], lsem.at[3]),
    ]
    for load in loads:
        load.start()

    def around(at, size):
        return [at] + [jnp.where(at + d >= size, at + d - size, at + d) for d in range(1, size)]

    zs, xs, ys = around(z, DEPTH), around(x, SIDE), around(y, SIDE)
    here = lax.axis_index("wide") - z
    x_low = [lax.rem(v, 2) * DEPTH + z for v in xs]
    x_high = [lax.div(v, 2) * CORES + core for v in xs]
    y_high = [v * (2 * CORES) for v in ys]
    mate = (here + z, n + 1 - 2 * core)
    z_peers = {d: (here + zs[d], n) for d in range(1, DEPTH)}
    p_peers = {
        q: (x_low[q // SIDE], x_high[q // SIDE] + y_high[q % SIDE]) for q in range(1, PLANE)
    }
    greeted = [mate, *p_peers.values()]
    greeted += [z_peers[d % DEPTH] for d in range(-REACH, REACH + 1) if d]
    barrier = pltpu.get_barrier_semaphore()
    for peer in greeted:
        pl.semaphore_signal(barrier, inc=1, device_id=peer, device_id_type=MESH)

    def remote(src, dst, send, recv, peer):
        return pltpu.make_async_remote_copy(
            src_ref=src, dst_ref=dst, send_sem=send, recv_sem=recv,
            device_id=peer, device_id_type=MESH,
        )

    def all_in(buffer, sem):
        remote(buffer, buffer, sem, sem, mate).wait_recv()

    def all_out(buffer, sem):
        remote(buffer, buffer, sem, sem, mate).wait_send()

    def opposite(q):
        return (-(q // SIDE)) % SIDE * SIDE + (-(q % SIDE)) % SIDE

    far_first = sorted(range(1, DEPTH), key=lambda d: -min(d, DEPTH - d))
    plane_far_first = sorted(range(1, PLANE), key=lambda q: -hops(q // SIDE) - hops(q % SIDE))

    loads[0].wait()
    mine = xb[pl.ds(n, 1), :]
    for k in range(xk):
        z1[NEAR, k : k + 1, :] = mine[:, k * lanes : (k + 1) * lanes]
    pl.semaphore_wait(barrier, len(greeted))

    def along_z(first, count, d, there, part):
        remote(
            z1.at[pl.ds(first, count)], z1.at[pl.ds(there, count)], az_s.at[0], az_r.at[part], z_peers[d % DEPTH]
        ).start()

    for d in (4, -4, 3, -3, 2, -2, 1, -1):
        slot = NEAR - d
        along_z(NEAR, 1, d, slot, 0 if slot < NEAR else 1 if slot < GROUP else 2)
    loads[2].wait()
    swap_c = remote(cc.at[0], cc.at[1], core_s.at[0], core_r.at[0], mate)
    swap_c.start()
    loads[3].wait()
    swap_w = remote(ww.at[0], ww.at[1], core_s.at[1], core_r.at[1], mate)
    swap_w.start()
    all_in(z1.at[pl.ds(0, 4)], az_r.at[0])
    along_z(0, 4, REACH, 12, 2)
    all_in(z1.at[pl.ds(5, 3)], az_r.at[1])
    along_z(5, 3, -REACH, 9, 2)

    for g in range(2):
        rows = slice(g * GROUP, (g + 1) * GROUP)
        here = pl.ds(g * GROUP, GROUP)
        if g == 1:
            all_in(z1.at[here], az_r.at[2])
        for k in range(xk):
            xa[0, rows, k * lanes : (k + 1) * lanes] = z1[rows, k, :]
        for q in plane_far_first:
            remote(xa.at[0, here], xa.at[opposite(q), here], ap_s.at[0], ap_r.at[g], p_peers[q]).start()

    loads[1].wait()
    swap_c.wait_recv()
    both = cc[...].reshape(2 * m, features)
    ones = jnp.ones((8, features), jnp.float32)
    cn[...] = lax.dot_general(
        ones, both * both, (((1,), (1,)), ((), ())), precision=HI, preferred_element_type=jnp.float32
    )
    ch[0], ch[1] = halves(both)
    swap_w.wait_recv()
    wh[0], wh[1] = halves(ww[...].reshape(2 * m, -1))

    kernels = []
    others = pl.ds(1, PLANE - 1)

    def send_parts(g):
        here = pl.ds(g * GROUP, GROUP)
        for q in plane_far_first:
            remote(pp.at[q, here], cb.at[opposite(q), here], cp_s.at[0], cp_r.at[g], p_peers[q]).start()

    for g in range(2):
        rows = slice(g * GROUP, (g + 1) * GROUP)
        all_in(xa.at[others, pl.ds(g * GROUP, GROUP)], ap_r.at[g])
        if g == 1:
            send_parts(0)
        points = xa[:, rows, :].reshape(PLANE * GROUP, features)
        norms = jnp.sum(points * points, axis=1, keepdims=True)
        cross = product(halves(points), (ch[0], ch[1]), ((1,), (1,)), True)
        kernel = jnp.exp(-(norms + cn[0:1, :] - 2.0 * cross) / features)
        kernel_halves = halves(kernel)
        part = product(kernel_halves, (wh[0], wh[1]), ((1,), (0,)), False)
        pp[:, rows, :] = part.reshape(PLANE, GROUP, -1)
        kernels.append(kernel)
    send_parts(1)
    for g in range(2):
        kt[g, 0], kt[g, 1] = halves(kernels[g].T)

    for g in range(2):
        rows = slice(g * GROUP, (g + 1) * GROUP)
        all_in(cb.at[others, pl.ds(g * GROUP, GROUP)], cp_r.at[g])
        total = pp[0, rows, :]
        for q in range(1, PLANE):
            total = total + cb[q, rows, :]
        for k in range(rk):
            s3[rows, k, :] = total[:, k * lanes : (k + 1) * lanes]
        for d in far_first:
            s = (NEAR + d) % DEPTH
            if s // GROUP == g:
                remote(s3.at[s], zb.at[DEPTH - 1 - d], cz_s.at[0], cz_r.at[0], z_peers[d]).start()

    own = s3[NEAR]
    all_in(zb, cz_r.at[0])
    for s in range(DEPTH - 1):
        own = own + zb[s]
    own = own * pred_scale
    for k in range(rk):
        piece = own[k : k + 1, :] - tg[:, k * lanes : (k + 1) * lanes]
        rz[NEAR, k : k + 1, :] = piece
        res_ref[:, k * lanes : (k + 1) * lanes] = piece

    for d in far_first:
        slot = (NEAR - d) % DEPTH
        remote(rz.at[NEAR], rz.at[slot], dz_s.at[0], dz_r.at[slot // GROUP], z_peers[d]).start()

    for g in range(2):
        rows = slice(g * GROUP, (g + 1) * GROUP)
        here = pl.ds(g * GROUP, GROUP)
        all_in(rz.at[pl.ds(g * GROUP, GROUP - 1 + g)], dz_r.at[g])
        for k in range(rk):
            rb[0, rows, k * lanes : (k + 1) * lanes] = rz[rows, k, :]
        for q in plane_far_first:
            remote(rb.at[0, here], rb.at[opposite(q), here], dp_s.at[0], dp_r.at[g], p_peers[q]).start()

    def update_part(g, residual, lo, cols):
        return product(
            (kt[g, 0, lo : lo + m, :], kt[g, 1, lo : lo + m, :]),
            tuple(half[:, cols] for half in residual), ((1,), (0,)), False,
        )

    parts = [slice(c * (rk * lanes // 2), (c + 1) * (rk * lanes // 2)) for c in range(2)]
    for g in range(2):
        all_in(rb.at[others, pl.ds(g * GROUP, GROUP)], dp_r.at[g])
        residual = halves(rb[:, g * GROUP : (g + 1) * GROUP, :].reshape(PLANE * GROUP, -1))
        if g == 0:
            for c in range(2):
                uu[c] = update_part(g, residual, m, parts[c])
            new_ref[...] = ww[0] - step * update_part(g, residual, 0, slice(None))
    swap_u = []
    for c in range(2):
        uu[c] = uu[c] + update_part(1, residual, m, parts[c])
        swap_u.append(remote(uu.at[c], ub.at[c], core_s.at[2 + c], core_r.at[2 + c], mate))
        swap_u[c].start()
    for c in range(2):
        own_part = new_ref[:, parts[c]] - step * update_part(1, residual, 0, parts[c])
        swap_u[c].wait_recv()
        new_ref[:, parts[c]] = own_part - step * ub[c]

    for swap in (swap_c, swap_w, *swap_u):
        swap.wait_send()
    all_out(z1.at[pl.ds(0, DEPTH - 1)], az_s.at[0])
    all_out(xa.at[others], ap_s.at[0])
    all_out(pp.at[others], cp_s.at[0])
    all_out(zb, cz_s.at[0])
    all_out(rz.at[pl.ds(0, DEPTH - 1)], dz_s.at[0])
    all_out(rb.at[others], dp_s.at[0])


def place_outputs(res_ref, new_ref, res_out, new_out, sems):
    copies = [
        pltpu.make_async_copy(new_ref, new_out, sems.at[0]),
        pltpu.make_async_copy(res_ref, res_out, sems.at[1]),
    ]
    for copy in copies:
        copy.start()
    for copy in copies:
        copy.wait()


def shards(batch, targets, centers, weights):
    m, features = centers.shape
    outputs = weights.shape[1]
    devices = lax.axis_size("wide") * lax.axis_size("narrow")
    all_rows = batch.shape[0] * lax.axis_size("wide")
    pred_scale = 8.0 / math.sqrt(m * devices)
    f32, bf16 = jnp.float32, jnp.bfloat16
    vmem = pltpu.VMEM
    dma = pltpu.SemaphoreType.DMA
    xk, rk = features // 128, outputs // 128
    scratch = [
        vmem(batch.shape, f32),
        vmem(targets.shape, f32),
        vmem((2, m, features), f32),
        vmem((2, m, outputs), f32),
        vmem((2, 2 * m, features), bf16),
        vmem((2, 2 * m, outputs), bf16),
        vmem((DEPTH, xk, 128), f32),
        vmem((PLANE, DEPTH, features), f32),
        vmem((8, 2 * m), f32),
        vmem((2, 2, 2 * m, PLANE * GROUP), bf16),
        vmem((PLANE, DEPTH, outputs), f32),
        vmem((PLANE, DEPTH, outputs), f32),
        vmem((DEPTH, rk, 128), f32),
        vmem((DEPTH - 1, rk, 128), f32),
        vmem((DEPTH, rk, 128), f32),
        vmem((PLANE, DEPTH, outputs), f32),
        vmem((2, m, outputs // 2), f32),
        vmem((2, m, outputs // 2), f32),
        dma((4,)),
        dma((4,)), dma((4,)),
        dma((1,)), dma((3,)),
        dma((1,)), dma((2,)),
        dma((1,)), dma((2,)),
        dma((1,)), dma((1,)),
        dma((1,)), dma((2,)),
        dma((1,)), dma((2,)),
    ]
    outputs_made = pl.pallas_call(
        functools.partial(body, pred_scale, 32.0 / all_rows),
        out_shape=(
            jax.ShapeDtypeStruct(targets.shape, f32),
            jax.ShapeDtypeStruct(weights.shape, f32),
        ),
        in_specs=[pl.BlockSpec(memory_space=pltpu.HBM)] * 4,
        out_specs=(pl.BlockSpec(memory_space=pltpu.VMEM),) * 2,
        scratch_shapes=scratch,
        compiler_params=pltpu.CompilerParams(
            collective_id=0, has_side_effects=True, vmem_limit_bytes=48 << 20
        ),
    )(*(pltpu.with_memory_space_constraint(a, pltpu.HBM) for a in (batch, targets, centers, weights)))
    return pl.pallas_call(
        place_outputs,
        out_shape=(
            jax.ShapeDtypeStruct(targets.shape, f32),
            jax.ShapeDtypeStruct(weights.shape, f32),
        ),
        in_specs=[pl.BlockSpec(memory_space=pltpu.VMEM)] * 2,
        out_specs=(pl.BlockSpec(memory_space=pltpu.HBM),) * 2,
        scratch_shapes=[dma((2,))],
        compiler_params=pltpu.CompilerParams(vmem_limit_bytes=8 << 20),
    )(*outputs_made)


def solution(mesh):
    both = P(("wide", "narrow"), None)
    return jax.shard_map(
        shards, mesh=mesh, in_specs=(P("wide", None), both, both, both), out_specs=(both, both), check_vma=False
    )
```

```python
import functools
import math

import jax
import jax.numpy as jnp
from jax import lax
from jax.experimental import pallas as pl
from jax.experimental.pallas import tpu as pltpu
from jax.sharding import PartitionSpec as P

SIDE, DEPTH, CORES = 4, 16, 2
PLANE = SIDE * SIDE
GROUP = 8
REACH = 4
NEAR = 4
MESH = pl.DeviceIdType.MESH
HI = lax.Precision.HIGHEST


def place():
    w, n = lax.axis_index("wide"), lax.axis_index("narrow")
    core, rest = lax.rem(n, CORES), lax.div(n, CORES)
    x_lo, z = lax.div(w, DEPTH), lax.rem(w, DEPTH)
    x_hi, y = lax.rem(rest, 2), lax.div(rest, 2)
    return x_hi * 2 + x_lo, y, z, core, n


def name_of(x, y, z, core):
    return (lax.rem(x, 2) * DEPTH + z, (y * 2 + lax.div(x, 2)) * CORES + core)


def halves(v):
    top = v.astype(jnp.bfloat16)
    return top, (v - top.astype(jnp.float32)).astype(jnp.bfloat16)


def product(a, b, dims, last):
    def dot(u, v):
        return lax.dot_general(u, v, (dims, ((), ())), preferred_element_type=jnp.float32)

    low = dot(a[0], b[1]) + dot(a[1], b[0])
    if last:
        low = low + dot(a[1], b[1])
    return dot(a[0], b[0]) + low


def hops(d):
    return min(d, SIDE - d)


def body(
    pred_scale, step, batch_ref, targets_ref, centers_ref, weights_ref, res_ref, new_ref,
    xb, tg, cc, ww, ch, wh, z1, xa, cn, kt, pp, cb, s3, zb, rz, rb, uu, ub,
    lsem, core_s, core_r, az_s, az_r, ap_s, ap_r, cp_s, cp_r, cz_s, cz_r, dz_s, dz_r, dp_s, dp_r,
):
    x, y, z, core, n = place()
    features = cc.shape[2]
    m = cc.shape[1]
    lanes = 128
    xk = features // lanes
    rk = rb.shape[2] // lanes

    loads = [
        pltpu.make_async_copy(batch_ref, xb, lsem.at[0]),
        pltpu.make_async_copy(targets_ref, tg, lsem.at[1]),
        pltpu.make_async_copy(centers_ref, cc.at[0], lsem.at[2]),
        pltpu.make_async_copy(weights_ref, ww.at[0], lsem.at[3]),
    ]
    loads[0].start()

    def around(at, size):
        return [at] + [jnp.where(at + d >= size, at + d - size, at + d) for d in range(1, size)]

    zs, xs, ys = around(z, DEPTH), around(x, SIDE), around(y, SIDE)
    here = lax.axis_index("wide") - z
    x_low = [lax.rem(v, 2) * DEPTH + z for v in xs]
    x_high = [lax.div(v, 2) * CORES + core for v in xs]
    y_high = [v * (2 * CORES) for v in ys]
    mate = (here + z, n + 1 - 2 * core)
    z_peers = {d: (here + zs[d], n) for d in range(1, DEPTH)}
    p_peers = {
        q: (x_low[q // SIDE], x_high[q // SIDE] + y_high[q % SIDE]) for q in range(1, PLANE)
    }
    greeted = [z_peers[d % DEPTH] for d in (4, -4, 3, -3, 2, -2, 1, -1)]
    greeted += [p_peers[q] for q in sorted(p_peers, key=lambda q: -hops(q // SIDE) - hops(q % SIDE))]
    greeted.append(mate)
    barrier = pltpu.get_barrier_semaphore()
    for peer in greeted:
        pl.semaphore_signal(barrier, inc=1, device_id=peer, device_id_type=MESH)
    for load in loads[1:]:
        load.start()

    def remote(src, dst, send, recv, peer):
        return pltpu.make_async_remote_copy(
            src_ref=src, dst_ref=dst, send_sem=send, recv_sem=recv,
            device_id=peer, device_id_type=MESH,
        )

    def all_in(buffer, sem):
        remote(buffer, buffer, sem, sem, mate).wait_recv()

    def all_out(buffer, sem):
        remote(buffer, buffer, sem, sem, mate).wait_send()

    def opposite(q):
        return (-(q // SIDE)) % SIDE * SIDE + (-(q % SIDE)) % SIDE

    far_first = sorted(range(1, DEPTH), key=lambda d: -min(d, DEPTH - d))
    plane_far_first = sorted(range(1, PLANE), key=lambda q: -hops(q // SIDE) - hops(q % SIDE))

    loads[0].wait()
    mine = xb[pl.ds(n, 1), :]
    for k in range(xk):
        z1[NEAR, k : k + 1, :] = mine[:, k * lanes : (k + 1) * lanes]
    pl.semaphore_wait(barrier, len(greeted))

    def along_z(first, count, d, there, part):
        remote(
            z1.at[pl.ds(first, count)], z1.at[pl.ds(there, count)], az_s.at[0], az_r.at[part], z_peers[d % DEPTH]
        ).start()

    for d in (4, -4, 3, -3, 2, -2, 1, -1):
        slot = NEAR - d
        along_z(NEAR, 1, d, slot, 0 if slot < NEAR else 1 if slot < GROUP else 2)
    loads[2].wait()
    swap_c = remote(cc.at[0], cc.at[1], core_s.at[0], core_r.at[0], mate)
    swap_c.start()
    loads[3].wait()
    swap_w = remote(ww.at[0], ww.at[1], core_s.at[1], core_r.at[1], mate)
    swap_w.start()
    all_in(z1.at[pl.ds(0, 4)], az_r.at[0])
    along_z(0, 4, REACH, 12, 2)
    all_in(z1.at[pl.ds(5, 3)], az_r.at[1])
    along_z(5, 3, -REACH, 9, 2)

    for g in range(2):
        rows = slice(g * GROUP, (g + 1) * GROUP)
        here = pl.ds(g * GROUP, GROUP)
        if g == 1:
            all_in(z1.at[here], az_r.at[2])
        for k in range(xk):
            xa[0, rows, k * lanes : (k + 1) * lanes] = z1[rows, k, :]
        for q in plane_far_first:
            remote(xa.at[0, here], xa.at[opposite(q), here], ap_s.at[0], ap_r.at[g], p_peers[q]).start()

    loads[1].wait()
    swap_c.wait_recv()
    both = cc[...].reshape(2 * m, features)
    ones = jnp.ones((8, features), jnp.float32)
    cn[...] = lax.dot_general(
        ones, both * both, (((1,), (1,)), ((), ())), precision=HI, preferred_element_type=jnp.float32
    )
    ch[0], ch[1] = halves(both)
    swap_w.wait_recv()
    wh[0], wh[1] = halves(ww[...].reshape(2 * m, -1))

    kernels = []
    others = pl.ds(1, PLANE - 1)

    def send_parts(g):
        here = pl.ds(g * GROUP, GROUP)
        for q in plane_far_first:
            remote(pp.at[q, here], cb.at[opposite(q), here], cp_s.at[0], cp_r.at[g], p_peers[q]).start()

    for g in range(2):
        rows = slice(g * GROUP, (g + 1) * GROUP)
        all_in(xa.at[others, pl.ds(g * GROUP, GROUP)], ap_r.at[g])
        if g == 1:
            send_parts(0)
        points = xa[:, rows, :].reshape(PLANE * GROUP, features)
        norms = jnp.sum(points * points, axis=1, keepdims=True)
        cross = product(halves(points), (ch[0], ch[1]), ((1,), (1,)), True)
        kernel = jnp.exp(-(norms + cn[0:1, :] - 2.0 * cross) / features)
        kernel_halves = halves(kernel)
        part = product(kernel_halves, (wh[0], wh[1]), ((1,), (0,)), False)
        pp[:, rows, :] = part.reshape(PLANE, GROUP, -1)
        kernels.append(kernel)
    send_parts(1)
    for g in range(2):
        kt[g, 0], kt[g, 1] = halves(kernels[g].T)

    for g in range(2):
        rows = slice(g * GROUP, (g + 1) * GROUP)
        all_in(cb.at[others, pl.ds(g * GROUP, GROUP)], cp_r.at[g])
        total = pp[0, rows, :]
        for q in range(1, PLANE):
            total = total + cb[q, rows, :]
        for k in range(rk):
            s3[rows, k, :] = total[:, k * lanes : (k + 1) * lanes]
        for d in far_first:
            s = (NEAR + d) % DEPTH
            if s // GROUP == g:
                remote(s3.at[s], zb.at[DEPTH - 1 - d], cz_s.at[0], cz_r.at[0], z_peers[d]).start()

    own = s3[NEAR]
    all_in(zb, cz_r.at[0])
    for s in range(DEPTH - 1):
        own = own + zb[s]
    own = own * pred_scale
    for k in range(rk):
        piece = own[k : k + 1, :] - tg[:, k * lanes : (k + 1) * lanes]
        rz[NEAR, k : k + 1, :] = piece
        res_ref[:, k * lanes : (k + 1) * lanes] = piece

    for d in far_first:
        slot = (NEAR - d) % DEPTH
        remote(rz.at[NEAR], rz.at[slot], dz_s.at[0], dz_r.at[slot // GROUP], z_peers[d]).start()

    for g in range(2):
        rows = slice(g * GROUP, (g + 1) * GROUP)
        here = pl.ds(g * GROUP, GROUP)
        all_in(rz.at[pl.ds(g * GROUP, GROUP - 1 + g)], dz_r.at[g])
        for k in range(rk):
            rb[0, rows, k * lanes : (k + 1) * lanes] = rz[rows, k, :]
        for q in plane_far_first:
            remote(rb.at[0, here], rb.at[opposite(q), here], dp_s.at[0], dp_r.at[g], p_peers[q]).start()

    def update_part(g, residual, lo, cols):
        return product(
            (kt[g, 0, lo : lo + m, :], kt[g, 1, lo : lo + m, :]),
            tuple(half[:, cols] for half in residual), ((1,), (0,)), False,
        )

    parts = [slice(c * (rk * lanes // 2), (c + 1) * (rk * lanes // 2)) for c in range(2)]
    for g in range(2):
        all_in(rb.at[others, pl.ds(g * GROUP, GROUP)], dp_r.at[g])
        residual = halves(rb[:, g * GROUP : (g + 1) * GROUP, :].reshape(PLANE * GROUP, -1))
        if g == 0:
            for c in range(2):
                uu[c] = update_part(g, residual, m, parts[c])
            new_ref[...] = ww[0] - step * update_part(g, residual, 0, slice(None))
    swap_u = []
    for c in range(2):
        uu[c] = uu[c] + update_part(1, residual, m, parts[c])
        swap_u.append(remote(uu.at[c], ub.at[c], core_s.at[2 + c], core_r.at[2 + c], mate))
        swap_u[c].start()
    for c in range(2):
        own_part = new_ref[:, parts[c]] - step * update_part(1, residual, 0, parts[c])
        swap_u[c].wait_recv()
        new_ref[:, parts[c]] = own_part - step * ub[c]

    for swap in (swap_c, swap_w, *swap_u):
        swap.wait_send()
    all_out(z1.at[pl.ds(0, DEPTH - 1)], az_s.at[0])
    all_out(xa.at[others], ap_s.at[0])
    all_out(pp.at[others], cp_s.at[0])
    all_out(zb, cz_s.at[0])
    all_out(rz.at[pl.ds(0, DEPTH - 1)], dz_s.at[0])
    all_out(rb.at[others], dp_s.at[0])


def place_outputs(res_ref, new_ref, res_out, new_out, sems):
    copies = [
        pltpu.make_async_copy(new_ref, new_out, sems.at[0]),
        pltpu.make_async_copy(res_ref, res_out, sems.at[1]),
    ]
    for copy in copies:
        copy.start()
    for copy in copies:
        copy.wait()


def shards(batch, targets, centers, weights):
    m, features = centers.shape
    outputs = weights.shape[1]
    devices = lax.axis_size("wide") * lax.axis_size("narrow")
    all_rows = batch.shape[0] * lax.axis_size("wide")
    pred_scale = 8.0 / math.sqrt(m * devices)
    f32, bf16 = jnp.float32, jnp.bfloat16
    vmem = pltpu.VMEM
    dma = pltpu.SemaphoreType.DMA
    xk, rk = features // 128, outputs // 128
    scratch = [
        vmem(batch.shape, f32),
        vmem(targets.shape, f32),
        vmem((2, m, features), f32),
        vmem((2, m, outputs), f32),
        vmem((2, 2 * m, features), bf16),
        vmem((2, 2 * m, outputs), bf16),
        vmem((DEPTH, xk, 128), f32),
        vmem((PLANE, DEPTH, features), f32),
        vmem((8, 2 * m), f32),
        vmem((2, 2, 2 * m, PLANE * GROUP), bf16),
        vmem((PLANE, DEPTH, outputs), f32),
        vmem((PLANE, DEPTH, outputs), f32),
        vmem((DEPTH, rk, 128), f32),
        vmem((DEPTH - 1, rk, 128), f32),
        vmem((DEPTH, rk, 128), f32),
        vmem((PLANE, DEPTH, outputs), f32),
        vmem((2, m, outputs // 2), f32),
        vmem((2, m, outputs // 2), f32),
        dma((4,)),
        dma((4,)), dma((4,)),
        dma((1,)), dma((3,)),
        dma((1,)), dma((2,)),
        dma((1,)), dma((2,)),
        dma((1,)), dma((1,)),
        dma((1,)), dma((2,)),
        dma((1,)), dma((2,)),
    ]
    outputs_made = pl.pallas_call(
        functools.partial(body, pred_scale, 32.0 / all_rows),
        out_shape=(
            jax.ShapeDtypeStruct(targets.shape, f32),
            jax.ShapeDtypeStruct(weights.shape, f32),
        ),
        in_specs=[pl.BlockSpec(memory_space=pltpu.HBM)] * 4,
        out_specs=(pl.BlockSpec(memory_space=pltpu.VMEM),) * 2,
        scratch_shapes=scratch,
        compiler_params=pltpu.CompilerParams(
            collective_id=0, has_side_effects=True, vmem_limit_bytes=48 << 20
        ),
    )(*(pltpu.with_memory_space_constraint(a, pltpu.HBM) for a in (batch, targets, centers, weights)))
    return pl.pallas_call(
        place_outputs,
        out_shape=(
            jax.ShapeDtypeStruct(targets.shape, f32),
            jax.ShapeDtypeStruct(weights.shape, f32),
        ),
        in_specs=[pl.BlockSpec(memory_space=pltpu.VMEM)] * 2,
        out_specs=(pl.BlockSpec(memory_space=pltpu.HBM),) * 2,
        scratch_shapes=[dma((2,))],
        compiler_params=pltpu.CompilerParams(vmem_limit_bytes=8 << 20),
    )(*outputs_made)


def solution(mesh):
    both = P(("wide", "narrow"), None)
    return jax.shard_map(
        shards, mesh=mesh, in_specs=(P("wide", None), both, both, both), out_specs=(both, both), check_vma=False
    )
```
